32 devices in a mesh: dp: 16 (over z, x, core), col: 2 (over y).
Axes of the slice: x: 2, y: 2, z: 4, core: 2. Of those that a mesh axis runs over, the one named last changes fastest.
Arguments:
- tokens: bfloat16 [2048, 2048], P('dp'), may hold values from -6 to 6
- routes: int32 [2048, 8], P('dp'), may hold values from 0 to 31, all different within a row; in each aligned block of 128 rows (0 to 127, 128 to 255, ...) at most 48 rows name the same one
- probs: float32 [2048, 8], P('dp'), may hold values from 0.1 to 1
- w_gate: bfloat16 [32, 2048, 768], P('dp', None, 'col'), may hold values from -0.125 to 0.125
- w_up: bfloat16 [32, 2048, 768], P('dp', None, 'col'), may hold values from -0.125 to 0.125
- w_down: bfloat16 [32, 768, 2048], P('dp', 'col'), may hold values from -0.21875 to 0.21875
- cotangent: bfloat16 [2048, 2048], P('dp', 'col'), may hold values from -6 to 6
Outputs:
- mixed: bfloat16 [2048, 2048], P('dp', 'col')
- grad_tokens: bfloat16 [2048, 2048], P('dp', 'col')
- grad_probs: float32 [2048, 8], P('dp')
- grad_gate: bfloat16 [32, 2048, 768], P('dp', None, 'col')
- grad_up: bfloat16 [32, 2048, 768], P('dp', None, 'col')
- grad_down: bfloat16 [32, 768, 2048], P('dp', 'col')
The draws below stay inside these ranges and needn't reach their ends.
Inputs may be any that keep to these rules, and one draw needn't show every extreme that they name: `routes`: each token names 8 different experts. Among the 128 tokens of one index of dp, no expert is named by more than 48 of them, a bound that some block reaches.
All inputs are finite; a program needn't handle non-finite values.
Results may differ from the reference program's by a relative error of at most 0.0064.
Values may be sent and summed in bfloat16 or wider, within the bound.
No kernel may reach another device: no remote copies, remote signals or barrier semaphores. Data moves between devices by JAX's collectives and lax.ppermute only.
A program may use at most 192 MiB of HBM per device.

```python
import math
import jax
import jax.numpy as jnp
import numpy as np
from jax import lax

D = 2048
HID = 768
TOP = 8
TOK_DEV = 128
EXPERTS = 32
CAP = 48
TOKENS = 2048
N_DP = 16


def shard_levels(own_key, dims, shards, low, largest):
    factor_of, own = 1.0, jax.random.fold_in(own_key, 6)
    for axis_at, blocks in shards:
        steps = jnp.exp(jax.random.uniform(jax.random.fold_in(own, axis_at), (blocks,), jnp.float32, low / len(shards), largest / len(shards)))
        factor_of = factor_of * jnp.repeat(steps, dims[axis_at] // blocks).reshape([-1 if axis == axis_at else 1 for axis in range(len(dims))])
    return factor_of


def routed_block(rng, own, number, rows, amount, top, reach, slope):
    ranking = jax.random.permutation(rng, amount)
    heavy_load, usual = portions_of(amount, rows * top, reach, slope, True), portions_of(amount, rows * top, reach, slope, False)
    places = jnp.arange(amount)

    def named(lengths, turn):
        used = int((lengths > 0).sum())
        fixed = max(1, used // 4)
        shifted = fixed + (places - fixed + turn * (used - fixed)) % max(1, amount - fixed)
        return jnp.zeros((amount,), jnp.int32).at[ranking[jnp.where(places < fixed, places, shifted)]].set(jnp.asarray(lengths, jnp.int32))

    lengths = jnp.where(number % 4 == 0, named(heavy_load, number // 4), named(usual, number - number // 4 - 1))
    mixed = jax.random.permutation(jax.random.fold_in(own, 3), amount)
    source_of, taker = mixed[0:amount // 2 * 2:2], mixed[1:amount // 2 * 2:2]
    slack = jnp.minimum(lengths[source_of] - 1, reach - lengths[taker]) // 2
    slack = jnp.where((source_of == ranking[0]) | (taker == ranking[0]) | (lengths[taker] == 0), 0, jnp.maximum(slack, 0))
    shifted = jax.random.randint(jax.random.fold_in(own, 4), (amount // 2,), 0, 1 << 20) % (slack + 1)
    lengths = lengths.at[source_of].add(-shifted).at[taker].add(shifted)
    items = jnp.searchsorted(jnp.cumsum(lengths), jnp.arange(rows * top), side="right").astype(jnp.int32)
    table = items.reshape(top, rows).T
    table = table[jax.random.permutation(jax.random.fold_in(own, 1), rows)]
    turn = jax.random.randint(jax.random.fold_in(own, 2), (rows, 1), 0, top)
    return jnp.take_along_axis(table, (jnp.arange(top)[None, :] + turn) % top, axis=1)


def portions_of(number_of, total, reach, slope, full):
    weights = [(1 << 20) // math.isqrt(rank ** slope) + 1 for rank in range(1, number_of + 1)]
    largest = reach if full else min(reach, max(-(-total // number_of), total * weights[0] // sum(weights)))
    least = 1 if total - largest >= number_of - 1 else 0
    counts, surplus = [largest] + [least] * (number_of - 1), total - largest - least * (number_of - 1)
    while surplus > 0:
        candidates = [i for i in range(1, number_of) if counts[i] < largest] or [i for i in range(1, number_of) if counts[i] < reach]
        whole, budget = sum([weights[i] for i in candidates]), surplus
        for i in candidates:
            extra = min(reach - counts[i], max(1, budget * weights[i] // whole), surplus)
            counts[i] = counts[i] + extra
            surplus = surplus - extra
    return np.array(counts)


def noise(stream_key, shape, deviation, most, cuts=(), held_as=jnp.bfloat16):
    entries = deviation * jax.random.normal(stream_key, shape, jnp.float32)
    if cuts:
        entries = entries * shard_levels(stream_key, shape, cuts, -0.22, 0.18)
    return jnp.clip(entries, -most, most).astype(held_as)


def setup_inputs(seed: int = 0) -> dict:
    key_of = jax.random.split(jax.random.key(seed), 8)
    tokens = noise(key_of[0], (TOKENS, D), 1.0, 6.0, ((0, 16),))
    routes_keys = jax.random.split(jax.random.fold_in(key_of[1], 1), TOKENS // TOK_DEV)
    routes_turns = jax.random.permutation(jax.random.fold_in(key_of[1], 3), TOKENS // TOK_DEV)
    routes = jax.vmap(lambda own, number: routed_block(jax.random.fold_in(key_of[1], 2), own, number, TOK_DEV, EXPERTS, TOP, CAP, 2))(routes_keys, routes_turns).reshape((TOKENS, TOP))
    probs = jnp.clip(0.1 + 0.9 * jax.random.uniform(key_of[2], (TOKENS, TOP), jnp.float32) ** shard_levels(key_of[2], (TOKENS, TOP), ((0, 16),), -0.2, 0.2), 0.1, 1.0)
    w_gate = noise(key_of[3], (EXPERTS, D, HID), D ** -0.5, 0.125, ((0, 16), (2, 2)))
    w_up = noise(key_of[4], (EXPERTS, D, HID), D ** -0.5, 0.125, ((0, 16), (2, 2)))
    w_down = noise(key_of[5], (EXPERTS, HID, D), HID ** -0.5, 0.21875, ((0, 16), (1, 2)))
    cotangent = noise(key_of[6], (TOKENS, D), 1.0, 6.0, ((0, 16), (1, 2)))
    return dict(tokens=tokens, routes=routes, probs=probs, w_gate=w_gate, w_up=w_up, w_down=w_down, cotangent=cotangent)


def slot_numbers(route_block):
    expert_ids = jnp.arange(EXPERTS, dtype=jnp.int32)
    onehot = (route_block[:, None] == expert_ids[None, :]).astype(jnp.int32)
    before = jnp.cumsum(onehot, axis=0) - onehot
    return jnp.sum(before * onehot, axis=1).astype(jnp.int32)


def reference(tokens, routes, probs, w_gate, w_up, w_down, cotangent):
    pair_count = TOK_DEV * TOP
    flat_routes = routes.reshape(N_DP, pair_count)
    slot_table = lax.map(slot_numbers, flat_routes)
    position = (flat_routes * CAP + slot_table).astype(jnp.int32)
    pair_ids = jnp.arange(N_DP * pair_count, dtype=jnp.int32).reshape(N_DP, pair_count)
    source_ids = jnp.arange(N_DP, dtype=jnp.int32)[:, None] + jnp.zeros((1, pair_count), jnp.int32)
    pair_table = jnp.full((N_DP, EXPERTS * CAP), -1, jnp.int32)
    pair_table = pair_table.at[source_ids, position].set(pair_ids)
    pair_table = pair_table.reshape(N_DP, EXPERTS, CAP).transpose(1, 0, 2).reshape(EXPERTS, N_DP * CAP)
    prob_flat = probs.reshape(-1)

    def one_expert(totals, inputs):
        mixed_acc, grad_acc, prob_acc = totals
        pair_list, gate_w, up_w, down_w = inputs
        is_valid = pair_list >= 0
        safe_pairs = jnp.where(is_valid, pair_list, 0).astype(jnp.int32)
        token_idx = (safe_pairs // TOP).astype(jnp.int32)
        pair_weight = jnp.where(is_valid, prob_flat[safe_pairs], 0.0 * prob_flat[0])
        row_block = jnp.where(is_valid[:, None], tokens[token_idx], jnp.zeros_like(tokens[:1]))
        gate_acts = jnp.dot(row_block, gate_w, preferred_element_type=jnp.float32)
        up_acts = jnp.dot(row_block, up_w, preferred_element_type=jnp.float32)
        sigmoid_g = jax.nn.sigmoid(gate_acts)
        silu_g = gate_acts * sigmoid_g
        hidden = (silu_g * up_acts).astype(jnp.bfloat16)
        out_rows = jnp.dot(hidden, down_w, preferred_element_type=jnp.float32).astype(jnp.bfloat16)
        cot_rows = cotangent[token_idx].astype(jnp.float32)
        d_out = (pair_weight[:, None] * cot_rows).astype(jnp.bfloat16)
        grad_down = jnp.dot(hidden.T, d_out, preferred_element_type=jnp.float32).astype(jnp.bfloat16)
        d_hidden = jnp.dot(d_out, down_w.T, preferred_element_type=jnp.float32)
        d_gate = (d_hidden * up_acts * sigmoid_g * (1.0 + gate_acts * (1.0 - sigmoid_g))).astype(jnp.bfloat16)
        d_up = (d_hidden * silu_g).astype(jnp.bfloat16)
        grad_gate = jnp.dot(row_block.T, d_gate, preferred_element_type=jnp.float32).astype(jnp.bfloat16)
        grad_up = jnp.dot(row_block.T, d_up, preferred_element_type=jnp.float32).astype(jnp.bfloat16)
        d_rows = (jnp.dot(d_gate, gate_w.T, preferred_element_type=jnp.float32)
                  + jnp.dot(d_up, up_w.T, preferred_element_type=jnp.float32)).astype(jnp.bfloat16)
        out_wide = out_rows.astype(jnp.float32)
        mixed_acc = mixed_acc.at[token_idx].add(pair_weight[:, None] * out_wide)
        grad_acc = grad_acc.at[token_idx].add(jnp.where(is_valid[:, None], d_rows.astype(jnp.float32), jnp.zeros_like(out_wide)))
        prob_terms = jnp.where(is_valid, jnp.sum(cot_rows * out_wide, axis=1), jnp.zeros_like(pair_weight))
        prob_acc = prob_acc.at[safe_pairs].add(prob_terms)
        return (mixed_acc, grad_acc, prob_acc), (grad_gate, grad_up, grad_down)

    start_totals = (jnp.zeros((TOKENS, D), jnp.float32), jnp.zeros((TOKENS, D), jnp.float32),
                    jnp.zeros((TOKENS * TOP,), jnp.float32))
    totals, grads = lax.scan(one_expert, start_totals, (pair_table, w_gate, w_up, w_down))
    mixed_acc, grad_acc, prob_acc = totals
    grad_gate, grad_up, grad_down = grads
    return (mixed_acc.astype(jnp.bfloat16), grad_acc.astype(jnp.bfloat16), prob_acc.reshape(TOKENS, TOP),
            grad_gate, grad_up, grad_down)
```

```python
import functools

import jax
import jax.numpy as jnp
from jax import lax
from jax.experimental import pallas as pl
from jax.experimental.pallas import tpu as pltpu
from jax.sharding import PartitionSpec as P

BF = jnp.bfloat16
F32 = jnp.float32
VMEM_BYTES = 60 * 1024 * 1024


def dot(a, b, dims):
    return lax.dot_general(a, b, ((dims[:1], dims[1:]), ((), ())), preferred_element_type=F32)


def round_kernel(col_ref, own, xother, cother, xcother, ypair, cypair, pe, wg, wu, wd,
                 xs, cs, hs, keep, send, gp,
                 x, c, wgv, wuv, wdv, h, outk, outs, sem_x, sem_c, sem_w, sem_o):
    rows = own.shape[0]
    width = x.shape[1]
    half = width // 2
    local, _, hid = wg.shape
    col = col_ref[0]
    mine = pl.multiple_of(col * half, half)
    theirs = pl.multiple_of((1 - col) * half, half)
    pieces = (own, xother, cother, xcother)
    x_copies, c_copies, w_copies = [], [], []

    def begin(src, dst, sem, into):
        copy = pltpu.make_async_copy(src, dst, sem)
        copy.start()
        into.append(copy)

    for e in range(local):
        begin(wg.at[e], wgv.at[:, pl.ds(e * hid, hid)], sem_w.at[e], w_copies)
    for b, piece in enumerate(pieces):
        begin(piece.at[:, pl.ds(0, width)], x.at[pl.ds(b * rows, rows), :], sem_x.at[b], x_copies)
    for e in range(local):
        begin(wu.at[e], wuv.at[:, pl.ds(e * hid, hid)], sem_w.at[local + e], w_copies)
    for b, piece in enumerate(pieces):
        pair = (ypair, cypair)[b // 2]
        begin(piece.at[:, pl.ds(width, half)], c.at[pl.ds(b * rows, rows), pl.ds(mine, half)],
              sem_c.at[b], c_copies)
        begin(pair.at[b % 2], c.at[pl.ds(b * rows, rows), pl.ds(theirs, half)],
              sem_c.at[4 + b], c_copies)
    for e in range(local):
        begin(wd.at[e], wdv.at[pl.ds(e * hid, hid), :], sem_w.at[2 * local + e], w_copies)

    for copy in x_copies + w_copies[:local]:
        copy.wait()
    out_x = pltpu.make_async_copy(x, xs, sem_o.at[0])
    out_x.start()
    gate = dot(x[...], wgv[...], (1, 0))
    for copy in w_copies[local:2 * local]:
        copy.wait()
    up = dot(x[...], wuv[...], (1, 0))
    for copy in c_copies + w_copies[2 * local:]:
        copy.wait()
    out_c = pltpu.make_async_copy(c, cs, sem_o.at[1])
    out_c.start()
    q = dot(c[...], wdv[...], (1, 1))
    total = local * hid
    for e in range(local):
        lo, hi = e * hid, (e + 1) * hid
        g, u, qe = gate[:, lo:hi], up[:, lo:hi], q[:, lo:hi]
        p = pe[:, e:e + 1]
        s = 1.0 / (1.0 + jnp.exp(-g))
        silu = g * s
        hidden = (silu * u).astype(BF).astype(F32)
        gp[:, e:e + 1] = jnp.sum(hidden * qe, axis=1, keepdims=True)
        dh = p * qe
        h[:, lo:hi] = (p * hidden).astype(BF)
        h[:, total + lo:total + hi] = (dh * u * s * (1.0 + g * (1.0 - s))).astype(BF)
        h[:, 2 * total + lo:2 * total + hi] = (dh * silu).astype(BF)
    out_h = pltpu.make_async_copy(h, hs, sem_o.at[2])
    out_h.start()
    for y, at in enumerate((mine, theirs)):
        part = dot(h[:, :total], wdv[:, pl.ds(at, half)], (1, 0)).astype(BF)
        for b in range(4):
            (outk, outs)[b // 2][y * 2 + b % 2] = part[b * rows:(b + 1) * rows]
    for y, at in enumerate((mine, theirs)):
        part = (dot(h[:, total:2 * total], wgv[pl.ds(at, half), :], (1, 1))
                + dot(h[:, 2 * total:], wuv[pl.ds(at, half), :], (1, 1))).astype(BF)
        for b in range(4):
            (outk, outs)[b // 2][4 + (b % 2) * 2 + y] = part[b * rows:(b + 1) * rows]
    out_s = pltpu.make_async_copy(outs, send, sem_o.at[3])
    out_s.start()
    out_k = pltpu.make_async_copy(outk, keep, sem_o.at[4])
    out_k.start()
    for copy in (out_x, out_c, out_h, out_s, out_k):
        copy.wait()


def one_round(col, pieces, pe, wg, wu, wd):
    rows = pieces[0].shape[0]
    local, width, hid = wg.shape
    total = local * hid
    half = width // 2
    n = 4 * rows
    anyspec = pl.BlockSpec(memory_space=pl.ANY)
    vspec = pl.BlockSpec(memory_space=pltpu.VMEM)
    return pl.pallas_call(
        round_kernel,
        in_specs=[pl.BlockSpec(memory_space=pltpu.SMEM)] + [anyspec] * 6 + [vspec] + [anyspec] * 3,
        out_specs=[anyspec] * 5 + [vspec],
        out_shape=[
            jax.ShapeDtypeStruct((n, width), BF),
            jax.ShapeDtypeStruct((n, width), BF),
            jax.ShapeDtypeStruct((n, 3 * total), BF),
            jax.ShapeDtypeStruct((8, rows, half), BF),
            jax.ShapeDtypeStruct((8, rows, half), BF),
            jax.ShapeDtypeStruct((n, local), F32),
        ],
        scratch_shapes=[
            pltpu.VMEM((n, width), BF),
            pltpu.VMEM((n, width), BF),
            pltpu.VMEM((width, total), BF),
            pltpu.VMEM((width, total), BF),
            pltpu.VMEM((total, width), BF),
            pltpu.VMEM((n, 3 * total), BF),
            pltpu.VMEM((8, rows, half), BF),
            pltpu.VMEM((8, rows, half), BF),
            pltpu.SemaphoreType.DMA((4,)),
            pltpu.SemaphoreType.DMA((8,)),
            pltpu.SemaphoreType.DMA((3 * local,)),
            pltpu.SemaphoreType.DMA((5,)),
        ],
        compiler_params=pltpu.CompilerParams(vmem_limit_bytes=VMEM_BYTES),
        cost_estimate=pl.CostEstimate(
            flops=12 * n * width * total, bytes_accessed=2 * (3 * total * width + 6 * n * width),
            transcendentals=n * total),
        name="moe_round",
    )(col, *pieces, pe, wg, wu, wd)


def wgrad_in_kernel(rounds, first, *refs):
    xs, hs, out = refs[:rounds], refs[rounds:2 * rounds], refs[2 * rounds]
    local, _, hid = out.shape
    acc = None
    for x, h in zip(xs, hs):
        term = dot(x[...], h[...], (0, 0))
        acc = term if acc is None else acc + term
    for e in range(local):
        out[e] = acc[:, e * hid:(e + 1) * hid].astype(BF)


def wgrad_in(xs, hs, first, local, hid):
    n, width = xs[0].shape
    total = local * hid
    blk = 512
    rounds = len(xs)
    return pl.pallas_call(
        functools.partial(wgrad_in_kernel, rounds, first),
        grid=(width // blk,),
        in_specs=[pl.BlockSpec((n, blk), lambda j: (0, j))] * rounds
        + [pl.BlockSpec((n, total), lambda j: (0, first))] * rounds,
        out_specs=pl.BlockSpec((local, blk, hid), lambda j: (0, j, 0)),
        out_shape=jax.ShapeDtypeStruct((local, width, hid), BF),
        compiler_params=pltpu.CompilerParams(vmem_limit_bytes=VMEM_BYTES),
        cost_estimate=pl.CostEstimate(
            flops=2 * rounds * n * width * total,
            bytes_accessed=2 * (rounds * n * (width + total) + width * total), transcendentals=0),
        name="grad_in",
    )(*xs, *hs)


def wgrad_down_kernel(rounds, *refs):
    cs, hs, out = refs[:rounds], refs[rounds:2 * rounds], refs[2 * rounds]
    local, hid, _ = out.shape
    acc = None
    for c, h in zip(cs, hs):
        term = dot(h[...], c[...], (0, 0))
        acc = term if acc is None else acc + term
    for e in range(local):
        out[e] = acc[e * hid:(e + 1) * hid].astype(BF)


def wgrad_down(cs, hs, local, hid):
    n, width = cs[0].shape
    total = local * hid
    blk = 512
    rounds = len(cs)
    return pl.pallas_call(
        functools.partial(wgrad_down_kernel, rounds),
        grid=(width // blk,),
        in_specs=[pl.BlockSpec((n, blk), lambda j: (0, j))] * rounds
        + [pl.BlockSpec((n, total), lambda j: (0, 0))] * rounds,
        out_specs=pl.BlockSpec((local, hid, blk), lambda j: (0, 0, j)),
        out_shape=jax.ShapeDtypeStruct((local, hid, width), BF),
        compiler_params=pltpu.CompilerParams(vmem_limit_bytes=VMEM_BYTES),
        cost_estimate=pl.CostEstimate(
            flops=2 * rounds * n * width * total,
            bytes_accessed=2 * (rounds * n * (width + total) + width * total), transcendentals=0),
        name="grad_down",
    )(*cs, *hs)


def dense_probs(routes, probs, experts):
    onehot = routes[:, :, None] == jnp.arange(experts, dtype=jnp.int32)
    return jnp.sum(jnp.where(onehot, probs[:, :, None], 0.0), axis=1), onehot


def add(*terms):
    return functools.reduce(lambda a, b: a + b, [t.astype(F32) for t in terms]).astype(BF)


def body16(tokens, routes, probs, w_gate, w_up, w_down, cotangent):
    rows, width = tokens.shape
    half = width // 2
    local, _, hid = w_gate.shape
    owners = lax.axis_size("dp")
    experts = local * owners
    place = lax.axis_index("dp")
    col = lax.axis_index("col")
    z, xc = place // 4, place % 4
    middle = (z == 1) | (z == 2)

    def permute(pairs):
        return lambda v: lax.ppermute(v, "dp", pairs)

    over_core = permute([(i, i ^ 1) for i in range(16)])
    over_x = permute([(i, i ^ 2) for i in range(16)])
    over_z = permute([(i, i ^ 4) for i in range(16)])
    across = permute([(4 + j, 8 + j) for j in range(4)] + [(8 + j, 4 + j) for j in range(4)])
    outward = permute([(4 + j, j) for j in range(4)] + [(8 + j, 12 + j) for j in range(4)])
    inward = permute([(j, 4 + j) for j in range(4)] + [(12 + j, 8 + j) for j in range(4)])

    def over_y(v):
        return lax.ppermute(v, "col", [(0, 1), (1, 0)])

    layer = jnp.stack([z, z ^ 1, jnp.where(z < 2, 2, 1), jnp.where(z < 2, 3, 0)])
    block = layer[:, None] * 4 + (xc ^ jnp.arange(4, dtype=jnp.int32)[jnp.array([0, 2, 1, 3])])[None, :]

    table, onehot = dense_probs(routes, probs, experts)
    arrived = lax.all_to_all(table.reshape(rows, owners, local).transpose(1, 0, 2), "dp", 0, 0, tiled=True)
    pe = arrived[block.reshape(-1)].reshape(4, 4 * rows, local)

    first = jnp.concatenate([tokens, cotangent], axis=1)
    second = over_z(first)
    third_near = across(first)
    fourth_near = across(second)
    third = jnp.where(middle, third_near, outward(third_near))
    fourth = jnp.where(middle, fourth_near, outward(fourth_near))

    colarr = col.reshape(1).astype(jnp.int32)
    done = []
    for r, own in enumerate((first, second, third, fourth)):
        xother = over_x(own)
        ypair = over_y(jnp.stack([own[:, width:], xother[:, width:]]))
        pieces = (own, xother, over_core(own), over_core(xother), ypair, over_core(ypair))
        done.append(one_round(colarr, pieces, pe[r], w_gate, w_up, w_down))

    sums = []
    for xs, cs, hs, keep, send, gp in done:
        got = over_core(send)
        m_keep, m_send = add(keep[0:2], got[0:2]), add(keep[2:4], got[2:4])
        g_keep, g_send = add(keep[4:6], got[4:6]), add(keep[6:8], got[6:8])
        m_got, g_got = over_y(m_send), over_x(g_send)
        m_keep, m_send = add(m_keep[0], m_got[0]), add(m_keep[1], m_got[1])
        g_keep, g_send = add(g_keep[0], g_got[0]), add(g_keep[1], g_got[1])
        m_got, g_got = over_x(m_send), over_y(g_send)
        sums.append(jnp.stack([add(m_keep, m_got), add(g_keep, g_got)]))

    far = across(add(sums[3], inward(sums[3])))
    mid = across(add(sums[2], inward(sums[2])))
    near = over_z(add(sums[1], far))
    result = add(sums[0], mid, near)

    gps = jnp.stack([d[5] for d in done]).reshape(16, rows, local)
    back = jnp.zeros_like(gps).at[block.reshape(-1)].set(gps)
    back = lax.all_to_all(back, "dp", 0, 0, tiled=True)
    back = lax.psum(back.transpose(1, 0, 2).reshape(rows, experts), "col")
    grad_probs = jnp.sum(jnp.where(onehot, back[:, None, :], 0.0), axis=2)

    xs, cs, hs = ([d[i] for d in done] for i in range(3))
    grad_down = wgrad_down(cs, hs, local, hid)
    grad_gate = wgrad_in(xs, hs, 1, local, hid)
    grad_up = wgrad_in(xs, hs, 2, local, hid)
    return result[0], result[1], grad_probs, grad_gate, grad_up, grad_down


def body_any(tokens, routes, probs, w_gate, w_up, w_down, cotangent):
    rows, width = tokens.shape
    half = width // 2
    local, _, hid = w_gate.shape
    owners = lax.axis_size("dp")
    experts = local * owners
    parts = max(1, rows * owners // 2048)
    step = rows // parts
    table, onehot = dense_probs(routes, probs, experts)
    arrived = lax.all_to_all(table.reshape(rows, owners, local).transpose(1, 0, 2), "dp", 0, 0, tiled=True)
    def one_part(grads, inputs):
        own_x, own_c, own_p = inputs
        x = lax.all_gather(own_x, "dp", axis=0, tiled=True)
        c = lax.all_gather(lax.all_gather(own_c, "dp", axis=0, tiled=True), "col", axis=1, tiled=True)
        p = own_p.reshape(owners * step, local).T[:, :, None]
        gate = jnp.einsum("td,ldh->lth", x, w_gate, preferred_element_type=F32)
        up = jnp.einsum("td,ldh->lth", x, w_up, preferred_element_type=F32)
        q = jnp.einsum("td,lhd->lth", c, w_down, preferred_element_type=F32)
        s = jax.nn.sigmoid(gate)
        silu = gate * s
        hidden = (silu * up).astype(BF).astype(F32)
        dh = p * q
        hp = (p * hidden).astype(BF)
        dg = (dh * up * s * (1.0 + gate * (1.0 - s))).astype(BF)
        du = (dh * silu).astype(BF)
        m = jnp.einsum("lth,lhd->td", hp, w_down, preferred_element_type=F32).astype(BF)
        g = (jnp.einsum("lth,ldh->td", dg, w_gate, preferred_element_type=F32)
             + jnp.einsum("lth,ldh->td", du, w_up, preferred_element_type=F32)).astype(BF)
        sums = []
        for part in (m, g):
            part = lax.psum_scatter(part, "dp", scatter_dimension=0, tiled=True)
            sums.append(lax.psum_scatter(part, "col", scatter_dimension=1, tiled=True))
        new = (jnp.einsum("td,lth->ldh", x, dg, preferred_element_type=F32),
               jnp.einsum("td,lth->ldh", x, du, preferred_element_type=F32),
               jnp.einsum("lth,td->lhd", hp, c, preferred_element_type=F32))
        grads = tuple(a + b for a, b in zip(grads, new))
        return grads, (*sums, jnp.sum(hidden * q, axis=2))

    zeros = tuple(jnp.zeros(w.shape, F32) for w in (w_gate, w_up, w_down))
    arrived = arrived.reshape(owners, parts, step, local).transpose(1, 0, 2, 3)
    grads, (mixed, grad_tokens, gps) = lax.scan(
        one_part, zeros,
        (tokens.reshape(parts, step, width), cotangent.reshape(parts, step, half), arrived))
    back = gps.reshape(parts, local, owners, step).transpose(2, 0, 3, 1).reshape(owners, rows, local)
    back = lax.all_to_all(back, "dp", 0, 0, tiled=True)
    back = lax.psum(back.transpose(1, 0, 2).reshape(rows, experts), "col")
    grad_probs = jnp.sum(jnp.where(onehot, back[:, None, :], 0.0), axis=2)
    return (mixed.reshape(rows, half), grad_tokens.reshape(rows, half), grad_probs,
            *(v.astype(BF) for v in grads))


def solution(mesh):
    body = body16 if mesh.shape["dp"] == 16 and mesh.shape["col"] == 2 else body_any
    return jax.shard_map(
        body,
        mesh=mesh,
        in_specs=(
            P("dp", None),
            P("dp", None),
            P("dp", None),
            P("dp", None, "col"),
            P("dp", None, "col"),
            P("dp", "col", None),
            P("dp", "col"),
        ),
        out_specs=(
            P("dp", "col"),
            P("dp", "col"),
            P("dp", None),
            P("dp", None, "col"),
            P("dp", None, "col"),
            P("dp", "col", None),
        ),
        check_vma=False,
    )
```

```python
import functools

import jax
import jax.numpy as jnp
from jax import lax
from jax.experimental import pallas as pl
from jax.experimental.pallas import tpu as pltpu
from jax.sharding import PartitionSpec as P

BF = jnp.bfloat16
F32 = jnp.float32
VMEM_BYTES = 60 * 1024 * 1024


def dot(a, b, dims):
    return lax.dot_general(a, b, ((dims[:1], dims[1:]), ((), ())), preferred_element_type=F32)


def begin(src, dst, sem, into):
    copy = pltpu.make_async_copy(src, dst, sem)
    copy.start()
    into.append(copy)


def rounds_kernel(cap, count, at_ref, *refs):
    groups = [refs[8 * i:8 * i + 8] for i in range(count)]
    blocks = [group[b] for group in groups for b in range(4)]
    others = [group[4 + b].at[b % 2 if group[4 + b].shape[0] == 2 else 0] for group in groups for b in range(4)]
    (wg, wu, wd, xs, cs, hs, keep, send, gp,
     x, c, tab, wgu, wdv, xp, cp, hp, mrow, grow, outk, outs,
     sem_x, sem_c, sem_t, sem_w, sem_o) = refs[8 * count:]
    rows = blocks[0].shape[0]
    pairs = 2 * count
    width = x.shape[1]
    half = width // 2
    local, _, hid = wg.shape
    wide = tab.shape[1]
    col = at_ref[0]
    first = at_ref[1]
    mine = pl.multiple_of(col * half, half)
    theirs = pl.multiple_of((1 - col) * half, half)
    x_copies, c_copies, t_copies, w_copies, o_copies = [], [], [], [], []

    for b, piece in enumerate(blocks):
        begin(piece.at[:, pl.ds(width + half, wide)], tab.at[pl.ds(b * rows, rows), :], sem_t.at[b], t_copies)
    for b, piece in enumerate(blocks):
        begin(piece.at[:, pl.ds(0, width)], x.at[pl.ds(b * rows, rows), :], sem_x.at[b], x_copies)
    for e in range(local):
        begin(wg.at[e], wgu.at[e, :, pl.ds(0, hid)], sem_w.at[3 * e], w_copies)
        begin(wu.at[e], wgu.at[e, :, pl.ds(hid, hid)], sem_w.at[3 * e + 1], w_copies)
    for b, piece in enumerate(blocks):
        begin(piece.at[:, pl.ds(width, half)], c.at[pl.ds(b * rows, rows), pl.ds(mine, half)],
              sem_c.at[b], c_copies)
        begin(others[b], c.at[pl.ds(b * rows, rows), pl.ds(theirs, half)],
              sem_c.at[4 * count + b], c_copies)
    for e in range(local):
        begin(wd.at[e], wdv.at[e], sem_w.at[3 * e + 2], w_copies)

    two = 2 * rows
    chunk = 2 * cap
    slots = local * chunk
    r_id = lax.broadcasted_iota(jnp.int32, (two, two), 0)
    c_id = lax.broadcasted_iota(jnp.int32, (two, two), 1)
    lower = ((c_id < r_id) & ((c_id < rows) == (r_id < rows))).astype(BF)
    lane = lax.broadcasted_iota(jnp.int32, (two, wide), 1)
    slot_id = lax.broadcasted_iota(jnp.int32, (two, slots), 1)
    base = jnp.where(lax.broadcasted_iota(jnp.int32, (two, 1), 0) < rows, 0, cap)
    s_lane = lax.broadcasted_iota(jnp.int32, (slots, wide), 1)
    s_row = lax.broadcasted_iota(jnp.int32, (slots, wide), 0)
    s_expert = first + s_row // chunk
    for copy in t_copies:
        copy.wait()
    picks, weights = [], []
    for k in range(pairs):
        values = tab[pl.ds(k * two, two), :]
        routed = values.astype(F32) > 0
        before = dot(lower, jnp.where(routed, 1.0, 0.0).astype(BF), (1, 0))
        pick = jnp.zeros((two, slots), F32)
        for e in range(local):
            here = (lane == first + e) & routed
            rank = jnp.sum(jnp.where(here, before + 1.0, 0.0), axis=1, keepdims=True).astype(jnp.int32)
            target = jnp.where(rank > 0, rank - 1 + e * chunk + base, -1)
            pick = pick + jnp.where(slot_id == target, 1.0, 0.0)
        pick = pick.astype(BF)
        picked = dot(pick, values, (0, 0))
        chosen = (s_lane == s_expert) | (s_lane == s_expert + wide // 2)
        picks.append(pick)
        weights.append(jnp.sum(jnp.where(chosen, picked, 0.0), axis=1, keepdims=True))

    def gather(src, dst):
        for k in range(pairs):
            part = dot(picks[k], src[pl.ds(k * two, two), :], (0, 0)).astype(BF)
            for e in range(local):
                dst[e, pl.ds(k * chunk, chunk), :] = part[e * chunk:(e + 1) * chunk]

    for copy in x_copies:
        copy.wait()
    gather(x, xp)
    begin(xp, xs, sem_o.at[0], o_copies)
    acts = []
    for e in range(local):
        w_copies[2 * e].wait()
        w_copies[2 * e + 1].wait()
        acts.append(dot(xp[e], wgu[e], (1, 0)))
    for copy in c_copies:
        copy.wait()
    gather(c, cp)
    begin(cp, cs, sem_o.at[1], o_copies)
    prods = []
    for e in range(local):
        w_copies[2 * local + e].wait()
        q = dot(cp[e], wdv[e], (1, 1))
        g, u = acts[e][:, :hid], acts[e][:, hid:]
        p = jnp.concatenate([w[e * chunk:(e + 1) * chunk] for w in weights], axis=0)
        s = 1.0 / (1.0 + jnp.exp(-g))
        silu = g * s
        hidden = (silu * u).astype(BF).astype(F32)
        prods.append(jnp.sum(hidden * q, axis=1, keepdims=True))
        dh = p * q
        hp[e, :, :hid] = (p * hidden).astype(BF)
        hp[e, :, hid:2 * hid] = (dh * u * s * (1.0 + g * (1.0 - s))).astype(BF)
        hp[e, :, 2 * hid:] = (dh * silu).astype(BF)
    begin(hp, hs, sem_o.at[2], o_copies)
    for e in range(local):
        out = dot(hp[e, :, :hid], wdv[e], (1, 0)).astype(BF)
        for k in range(pairs):
            mrow[k, pl.ds(e * chunk, chunk), :] = out[k * chunk:(k + 1) * chunk]
    for k in range(pairs):
        for y, at in enumerate((mine, theirs)):
            part = dot(picks[k], mrow[k, :, pl.ds(at, half)], (1, 0)).astype(BF)
            for b in range(2):
                (outk, outs)[k % 2][(y * 2 + b) * count + k // 2] = part[b * rows:(b + 1) * rows]
    for k in range(2):
        half_out = pl.ds(0, 4 * count)
        begin((outk, outs)[k].at[half_out], (keep, send)[k].at[half_out], sem_o.at[3 + k], o_copies)
    for e in range(local):
        out = dot(hp[e, :, hid:], wgu[e], (1, 1)).astype(BF)
        for k in range(pairs):
            grow[k, pl.ds(e * chunk, chunk), :] = out[k * chunk:(k + 1) * chunk]
    for k in (*range(1, pairs, 2), *range(0, pairs, 2)):
        for y, at in enumerate((mine, theirs)):
            part = dot(picks[k], grow[k, :, pl.ds(at, half)], (1, 0)).astype(BF)
            for b in range(2):
                (outk, outs)[k % 2][(4 + b * 2 + y) * count + k // 2] = part[b * rows:(b + 1) * rows]
        for b in range(4):
            slot = (4 + b) * count + k // 2
            begin((outk, outs)[k % 2].at[slot], (keep, send)[k % 2].at[slot], sem_o.at[5 + 4 * k + b], o_copies)
    for k in range(pairs):
        prod = jnp.concatenate([v[k * chunk:(k + 1) * chunk] for v in prods], axis=0)
        high = prod.astype(BF).astype(F32)
        spread = (jnp.where(s_lane == s_row // chunk, high, 0.0)
                  + jnp.where(s_lane == s_row // chunk + wide // 2, prod - high, 0.0)).astype(BF)
        both = dot(picks[k], spread, (1, 0)).T
        gp[:, pl.ds(k * two, two)] = both[:8] + both[wide // 2:wide // 2 + 8]
    for copy in o_copies:
        copy.wait()


def rounds(at, pieces, cap, wg, wu, wd):
    count = len(pieces) // 8
    rows = pieces[0].shape[0]
    local, width, hid = wg.shape
    half = width // 2
    n = count * 4 * rows
    wide = pieces[0].shape[1] - width - half
    packed = count * 4 * cap
    anyspec = pl.BlockSpec(memory_space=pl.ANY)
    vspec = pl.BlockSpec(memory_space=pltpu.VMEM)
    return pl.pallas_call(
        functools.partial(rounds_kernel, cap, count),
        in_specs=[pl.BlockSpec(memory_space=pltpu.SMEM)] + [anyspec] * (8 * count + 3),
        out_specs=[anyspec] * 5 + [vspec],
        out_shape=[
            jax.ShapeDtypeStruct((local, packed, width), BF),
            jax.ShapeDtypeStruct((local, packed, width), BF),
            jax.ShapeDtypeStruct((local, packed, 3 * hid), BF),
            jax.ShapeDtypeStruct((8 * count, rows, half), BF),
            jax.ShapeDtypeStruct((8 * count, rows, half), BF),
            jax.ShapeDtypeStruct((8, n), F32),
        ],
        scratch_shapes=[
            pltpu.VMEM((n, width), BF),
            pltpu.VMEM((n, width), BF),
            pltpu.VMEM((n, wide), BF),
            pltpu.VMEM((local, width, 2 * hid), BF),
            pltpu.VMEM((local, hid, width), BF),
            pltpu.VMEM((local, packed, width), BF),
            pltpu.VMEM((local, packed, width), BF),
            pltpu.VMEM((local, packed, 3 * hid), BF),
            pltpu.VMEM((2 * count, local * 2 * cap, width), BF),
            pltpu.VMEM((2 * count, local * 2 * cap, width), BF),
            pltpu.VMEM((8 * count, rows, half), BF),
            pltpu.VMEM((8 * count, rows, half), BF),
            pltpu.SemaphoreType.DMA((4 * count,)),
            pltpu.SemaphoreType.DMA((8 * count,)),
            pltpu.SemaphoreType.DMA((4 * count,)),
            pltpu.SemaphoreType.DMA((3 * local,)),
            pltpu.SemaphoreType.DMA((5 + 8 * count,)),
        ],
        compiler_params=pltpu.CompilerParams(vmem_limit_bytes=VMEM_BYTES),
        cost_estimate=pl.CostEstimate(
            flops=12 * local * packed * width * hid, bytes_accessed=2 * (3 * local * hid * width + 6 * n * width),
            transcendentals=local * packed * hid),
        name="moe_rounds",
    )(at, *pieces, wg, wu, wd)


def weight_kernel(rounds, off, outs_n, *refs):
    acts, hs = refs[:rounds], refs[rounds:2 * rounds]
    outs = refs[2 * rounds:2 * rounds + outs_n]
    a, h = refs[2 * rounds + outs_n:2 * rounds + outs_n + 2]
    stage = refs[2 * rounds + outs_n + 2:2 * rounds + 2 * outs_n + 2]
    sem_a, sem_h, sem_o = refs[2 * rounds + 2 * outs_n + 2:]
    local, total, width = a.shape
    packed = total // rounds
    cols = h.shape[2]
    hid = cols // outs_n
    copies, o_copies = [], []
    for e in range(local):
        mine = []
        for r in range(rounds):
            begin(hs[r].at[e, :, pl.ds(off, cols)], h.at[e, pl.ds(r * packed, packed), :], sem_h.at[e, r], mine)
            begin(acts[r].at[e], a.at[e, pl.ds(r * packed, packed), :], sem_a.at[e, r], mine)
        copies.append(mine)
    step = 512
    for e in range(local):
        for copy in copies[e]:
            copy.wait()
        for j in range(width // step):
            block = pl.ds(j * step, step)
            if outs_n == 2:
                grad = dot(a[e, :, block], h[e], (0, 0)).astype(BF)
                for i in range(outs_n):
                    stage[i][e, block, :] = grad[:, i * hid:(i + 1) * hid]
                    begin(stage[i].at[e, block], outs[i].at[e, block], sem_o.at[e, j, i], o_copies)
            else:
                stage[0][e, :, block] = dot(h[e], a[e, :, block], (0, 0)).astype(BF)
                begin(stage[0].at[e, :, block], outs[0].at[e, :, block], sem_o.at[e, j, 0], o_copies)
    for copy in o_copies:
        copy.wait()


def weight_grads(acts, hs, off, cols, outs_n, shape, name):
    local, packed, width = acts[0].shape
    rounds = len(acts)
    anyspec = pl.BlockSpec(memory_space=pl.ANY)
    return pl.pallas_call(
        functools.partial(weight_kernel, rounds, off, outs_n),
        in_specs=[anyspec] * (2 * rounds),
        out_specs=[anyspec] * outs_n,
        out_shape=[jax.ShapeDtypeStruct(shape, BF)] * outs_n,
        scratch_shapes=[
            pltpu.VMEM((local, rounds * packed, width), BF),
            pltpu.VMEM((local, rounds * packed, cols), BF),
            *[pltpu.VMEM(shape, BF)] * outs_n,
            pltpu.SemaphoreType.DMA((local, rounds)),
            pltpu.SemaphoreType.DMA((local, rounds)),
            pltpu.SemaphoreType.DMA((local, width // 512, outs_n)),
        ],
        compiler_params=pltpu.CompilerParams(vmem_limit_bytes=VMEM_BYTES),
        cost_estimate=pl.CostEstimate(
            flops=2 * local * rounds * packed * width * cols,
            bytes_accessed=2 * local * (rounds * packed * (width + cols) + width * cols), transcendentals=0),
        name=name,
    )(*acts, *hs)


def dense_probs(routes, probs, experts):
    onehot = routes[:, :, None] == jnp.arange(experts, dtype=jnp.int32)
    return jnp.sum(jnp.where(onehot, probs[:, :, None], 0.0), axis=1), onehot


def add(*terms):
    return functools.reduce(lambda a, b: a + b, [t.astype(F32) for t in terms])


sync = lax.optimization_barrier


def add16(*terms):
    return add(*terms).astype(BF)


def body16(tokens, routes, probs, w_gate, w_up, w_down, cotangent):
    rows, width = tokens.shape
    half = width // 2
    local, _, hid = w_gate.shape
    owners = lax.axis_size("dp")
    experts = local * owners
    place = lax.axis_index("dp")
    col = lax.axis_index("col")
    z = place // 4
    middle = (z == 1) | (z == 2)

    def permute(pairs):
        return lambda v: lax.ppermute(v, "dp", pairs)

    over_core = permute([(i, i ^ 1) for i in range(16)])
    over_x = permute([(i, i ^ 2) for i in range(16)])
    over_z = permute([(i, i ^ 4) for i in range(16)])
    across = permute([(4 + j, 8 + j) for j in range(4)] + [(8 + j, 4 + j) for j in range(4)])
    outward = permute([(4 + j, j) for j in range(4)] + [(8 + j, 12 + j) for j in range(4)])
    leap = permute([(4 * a + j, 4 * b + j) for a, b in ((0, 1), (3, 2), (1, 3), (2, 0)) for j in range(4)])
    end_to_end = permute([(j, 12 + j) for j in range(4)] + [(12 + j, j) for j in range(4)])

    def over_y(v):
        return lax.ppermute(v, "col", [(0, 1), (1, 0)])

    table, onehot = dense_probs(routes, probs, experts)
    high = table.astype(BF)
    low = (table - high.astype(F32)).astype(BF)
    gap = jnp.zeros((rows, 64 - experts), BF)
    first = jnp.concatenate([tokens, cotangent, high, gap, low, gap], axis=1)

    def pair(own, other):
        return jnp.stack([own[:, width:width + half], other[:, width:width + half]])

    cap = 3 * rows * routes.shape[1] // (2 * experts)
    at = jnp.stack([col, place * local]).astype(jnp.int32)

    def run(*pieces):
        return rounds(at, pieces, cap, w_gate, w_up, w_down)

    def stage_one(keep, got):
        return over_y(add16(keep[4:8], got[4:8])), over_x(add16(keep[12:16], got[12:16]))

    def stage_two(keep, got, m_got, g_got):
        return (over_x(add16(keep[2:4], got[2:4], m_got[2:4])),
                over_y(add16(keep[10:12], got[10:12], g_got[2:4])))

    def layer_sum(keep, got, one, two, r):
        return jnp.stack([add(keep[r], got[r], one[0][r], two[0][r]),
                          add(keep[8 + r], got[8 + r], one[1][r], two[1][r])])

    l0 = first
    l1, b1, x0 = over_z(l0), across(l0), over_x(l0)
    l0, l1, b1, x0 = sync((l0, l1, b1, x0))

    c1, b2, x1, y0 = across(l1), outward(b1), over_x(l1), over_y(pair(l0, x0))
    k0, kx0 = over_core(l0), over_core(x0)
    l0, l1, b1, b2, c1, x0, x1, y0 = sync((l0, l1, b1, b2, c1, x0, x1, y0))

    l2 = jnp.where(middle, c1, b2)
    c2, x2, y1 = outward(c1), over_x(l2), over_y(pair(l1, x1))
    k1, kx1, ky0 = over_core(l1), over_core(x1), over_core(y0)
    l2, c2, x2, y1 = sync((l2, c2, x2, y1))

    l3 = jnp.where(middle, b1, c2)
    x3, y2, y3 = over_x(l3), over_y(pair(l2, x2)), over_y(l3[None, :, width:width + half])
    ky1 = over_core(y1)
    k2, kx2, k3 = over_core(l2), over_core(x2), over_core(l3)
    xs_a, cs_a, hs_a, keep_a, send_a, gp_a = run(
        l0, x0, k0, kx0, y0, y0, ky0, ky0, l1, x1, k1, kx1, y1, y1, ky1, ky1)
    l2, x2, l3, x3, y2, y3, k2, kx2, k3, keep_a, send_a = sync(
        (l2, x2, l3, x3, y2, y3, k2, kx2, k3, keep_a, send_a))

    yx3 = over_y(x3[None, :, width:width + half])
    ky2, kx3, ky3 = over_core(y2), over_core(x3), over_core(y3)
    got_a = over_core(send_a)
    yx3, ky2, kx3, ky3, keep_a, got_a = sync((yx3, ky2, kx3, ky3, keep_a, got_a))

    kyx3 = over_core(yx3)
    one_a = stage_one(keep_a, got_a)
    xs_b, cs_b, hs_b, keep_b, send_b, gp_b = run(
        l2, x2, k2, kx2, y2, y2, ky2, ky2, l3, x3, k3, kx3, y3, yx3, ky3, kyx3)
    one_a, keep_b, send_b = sync((one_a, keep_b, send_b))

    got_b = over_core(send_b)
    two_a = stage_two(keep_a, got_a, *one_a)
    got_b, two_a = sync((got_b, two_a))

    one_b = stage_one(keep_b, got_b)
    from1 = over_z(layer_sum(keep_a, got_a, one_a, two_a, 1).astype(BF))
    grad_gate, grad_up = weight_grads([xs_a, xs_b], [hs_a, hs_b], hid, 2 * hid, 2, w_gate.shape, "grad_in")
    gps = jnp.concatenate([gp_a[:local], gp_b[:local]], axis=1).reshape(local, 4, 4, rows)
    gps = gps[:, :, jnp.array([0, 2, 1, 3])].reshape(local, owners, rows).transpose(1, 0, 2)
    gps = gps[jnp.arange(owners) ^ place]
    one_b, from1, grad_gate, grad_up, gps = sync((one_b, from1, grad_gate, grad_up, gps))

    two_b = stage_two(keep_b, got_b, *one_b)
    back = lax.all_to_all(gps, "dp", 0, 0, tiled=True)
    two_b, back = sync((two_b, back))

    sum2, sum3 = layer_sum(keep_b, got_b, one_b, two_b, 0).astype(BF), layer_sum(keep_b, got_b, one_b, two_b, 1)
    step, ends = leap(sum2), end_to_end(sum3.astype(BF))
    (grad_down,) = weight_grads([cs_a, cs_b], [hs_a, hs_b], 0, hid, 1, w_down.shape, "grad_down")
    other_back = over_y(back)
    sum3, step, ends, grad_down, other_back = sync((sum3, step, ends, grad_down, other_back))

    inner = across(add16(sum3, step))
    result = add16(layer_sum(keep_a, got_a, one_a, two_a, 0), from1, jnp.where(middle, inner, add16(step, ends)))

    back = (back + other_back).reshape(experts, rows).T
    grad_probs = jnp.sum(jnp.where(onehot, back[:, None, :], 0.0), axis=2)
    return result[0], result[1], grad_probs, grad_gate, grad_up, grad_down


def body_any(tokens, routes, probs, w_gate, w_up, w_down, cotangent):
    rows, width = tokens.shape
    half = width // 2
    local, _, hid = w_gate.shape
    owners = lax.axis_size("dp")
    experts = local * owners
    parts = max(1, rows * owners // 2048)
    step = rows // parts
    table, onehot = dense_probs(routes, probs, experts)
    arrived = lax.all_to_all(table.reshape(rows, owners, local).transpose(1, 0, 2), "dp", 0, 0, tiled=True)
    def one_part(grads, inputs):
        own_x, own_c, own_p = inputs
        x = lax.all_gather(own_x, "dp", axis=0, tiled=True)
        c = lax.all_gather(lax.all_gather(own_c, "dp", axis=0, tiled=True), "col", axis=1, tiled=True)
        p = own_p.reshape(owners * step, local).T[:, :, None]
        gate = jnp.einsum("td,ldh->lth", x, w_gate, preferred_element_type=F32)
        up = jnp.einsum("td,ldh->lth", x, w_up, preferred_element_type=F32)
        q = jnp.einsum("td,lhd->lth", c, w_down, preferred_element_type=F32)
        s = jax.nn.sigmoid(gate)
        silu = gate * s
        hidden = (silu * up).astype(BF).astype(F32)
        dh = p * q
        hp = (p * hidden).astype(BF)
        dg = (dh * up * s * (1.0 + gate * (1.0 - s))).astype(BF)
        du = (dh * silu).astype(BF)
        m = jnp.einsum("lth,lhd->td", hp, w_down, preferred_element_type=F32).astype(BF)
        g = (jnp.einsum("lth,ldh->td", dg, w_gate, preferred_element_type=F32)
             + jnp.einsum("lth,ldh->td", du, w_up, preferred_element_type=F32)).astype(BF)
        sums = []
        for part in (m, g):
            part = lax.psum_scatter(part, "dp", scatter_dimension=0, tiled=True)
            sums.append(lax.psum_scatter(part, "col", scatter_dimension=1, tiled=True))
        new = (jnp.einsum("td,lth->ldh", x, dg, preferred_element_type=F32),
               jnp.einsum("td,lth->ldh", x, du, preferred_element_type=F32),
               jnp.einsum("lth,td->lhd", hp, c, preferred_element_type=F32))
        grads = tuple(a + b for a, b in zip(grads, new))
        return grads, (*sums, jnp.sum(hidden * q, axis=2))

    zeros = tuple(jnp.zeros(w.shape, F32) for w in (w_gate, w_up, w_down))
    arrived = arrived.reshape(owners, parts, step, local).transpose(1, 0, 2, 3)
    grads, (mixed, grad_tokens, gps) = lax.scan(
        one_part, zeros,
        (tokens.reshape(parts, step, width), cotangent.reshape(parts, step, half), arrived))
    back = gps.reshape(parts, local, owners, step).transpose(2, 0, 3, 1).reshape(owners, rows, local)
    back = lax.all_to_all(back, "dp", 0, 0, tiled=True)
    back = lax.psum(back.transpose(1, 0, 2).reshape(rows, experts), "col")
    grad_probs = jnp.sum(jnp.where(onehot, back[:, None, :], 0.0), axis=2)
    return (mixed.reshape(rows, half), grad_tokens.reshape(rows, half), grad_probs,
            *(v.astype(BF) for v in grads))


def solution(mesh):
    body = body16 if mesh.shape["dp"] == 16 and mesh.shape["col"] == 2 else body_any
    return jax.shard_map(
        body,
        mesh=mesh,
        in_specs=(
            P("dp", None),
            P("dp", None),
            P("dp", None),
            P("dp", None, "col"),
            P("dp", None, "col"),
            P("dp", "col", None),
            P("dp", "col"),
        ),
        out_specs=(
            P("dp", "col"),
            P("dp", "col"),
            P("dp", None),
            P("dp", None, "col"),
            P("dp", None, "col"),
            P("dp", "col", None),
        ),
        check_vma=False,
    )
```

```python
import functools

import jax
import jax.numpy as jnp
from jax import lax
from jax.experimental import pallas as pl
from jax.experimental.pallas import tpu as pltpu
from jax.sharding import PartitionSpec as P

BF = jnp.bfloat16
F32 = jnp.float32


def dot(a, b, dims):
    return lax.dot_general(a, b, ((dims[:1], dims[1:]), ((), ())), preferred_element_type=F32)


def begin(src, dst, sem, into):
    copy = pltpu.make_async_copy(src, dst, sem)
    copy.start()
    into.append(copy)


def rounds_kernel(cap, count, at_ref, *refs):
    groups = [refs[8 * i:8 * i + 8] for i in range(count)]
    blocks = [group[b] for group in groups for b in range(4)]
    others = [group[4 + b].at[b % 2 if group[4 + b].shape[0] == 2 else 0] for group in groups for b in range(4)]
    (wg, wu, wd, xs, cs, hs, keep, send, gp,
     x, c, tab, wgu, wdv, xp, cp, hp, row,
     sem_x, sem_c, sem_t, sem_w, sem_o) = refs[8 * count:]
    rows = blocks[0].shape[0]
    pairs = 2 * count
    local, width, hid = wg.shape
    half = width // 2
    outk, outs = x, c
    wide = tab.shape[1]
    col = at_ref[0]
    first = at_ref[1]
    mine = pl.multiple_of(col * half, half)
    theirs = pl.multiple_of((1 - col) * half, half)
    held = 4 * count
    x_copies, c_copies, t_copies, w_copies, o_copies = [], [], [], [], []

    for b, piece in enumerate(blocks):
        begin(piece.at[:, pl.ds(width + half, wide)], tab.at[pl.ds(b * rows, rows), :], sem_t.at[b], t_copies)
    for b, piece in enumerate(blocks):
        for y in range(2):
            begin(piece.at[:, pl.ds(y * half, half)], x.at[y * held + b], sem_x.at[y * held + b], x_copies)
    for e in range(local):
        begin(wg.at[e], wgu.at[e, :, pl.ds(0, hid)], sem_w.at[3 * e], w_copies)
        begin(wu.at[e], wgu.at[e, :, pl.ds(hid, hid)], sem_w.at[3 * e + 1], w_copies)
    for b, piece in enumerate(blocks):
        begin(piece.at[:, pl.ds(width, half)], c.at[col * held + b], sem_c.at[b], c_copies)
        begin(others[b], c.at[(1 - col) * held + b], sem_c.at[held + b], c_copies)
    for e in range(local):
        begin(wd.at[e], wdv.at[e], sem_w.at[3 * e + 2], w_copies)

    two = 2 * rows
    chunk = 2 * cap
    slots = local * chunk
    r_id = lax.broadcasted_iota(jnp.int32, (two, two), 0)
    c_id = lax.broadcasted_iota(jnp.int32, (two, two), 1)
    lower = ((c_id < r_id) & ((c_id < rows) == (r_id < rows))).astype(BF)
    lane = lax.broadcasted_iota(jnp.int32, (two, wide), 1)
    slot_id = lax.broadcasted_iota(jnp.int32, (two, slots), 1)
    base = jnp.where(lax.broadcasted_iota(jnp.int32, (two, 1), 0) < rows, 0, cap)
    s_lane = lax.broadcasted_iota(jnp.int32, (slots, wide), 1)
    s_row = lax.broadcasted_iota(jnp.int32, (slots, wide), 0)
    s_expert = first + s_row // chunk
    for copy in t_copies:
        copy.wait()
    picks, weights = [], []
    for k in range(pairs):
        values = tab[pl.ds(k * two, two), :]
        routed = values.astype(F32) > 0
        before = dot(lower, jnp.where(routed, 1.0, 0.0).astype(BF), (1, 0))
        pick = jnp.zeros((two, slots), F32)
        for e in range(local):
            here = (lane == first + e) & routed
            rank = jnp.sum(jnp.where(here, before + 1.0, 0.0), axis=1, keepdims=True).astype(jnp.int32)
            target = jnp.where(rank > 0, rank - 1 + e * chunk + base, -1)
            pick = pick + jnp.where(slot_id == target, 1.0, 0.0)
        pick = pick.astype(BF)
        picked = dot(pick, values, (0, 0))
        chosen = (s_lane == s_expert) | (s_lane == s_expert + wide // 2)
        picks.append(pick)
        weights.append(jnp.sum(jnp.where(chosen, picked, 0.0), axis=1, keepdims=True))

    def gather(src, dst):
        for k in range(pairs):
            for y in range(2):
                part = dot(picks[k], src[pl.ds(y * held + 2 * k, 2)].reshape(two, half), (0, 0)).astype(BF)
                for e in range(local):
                    dst[e, pl.ds(k * chunk, chunk), pl.ds(y * half, half)] = part[e * chunk:(e + 1) * chunk]

    for copy in x_copies:
        copy.wait()
    gather(x, xp)
    begin(xp, xs, sem_o.at[0], o_copies)
    acts = []
    for e in range(local):
        w_copies[2 * e].wait()
        w_copies[2 * e + 1].wait()
        acts.append(dot(xp[e], wgu[e], (1, 0)))
    for copy in c_copies:
        copy.wait()
    gather(c, cp)
    begin(cp, cs, sem_o.at[1], o_copies)
    prods = []
    for e in range(local):
        w_copies[2 * local + e].wait()
        q = dot(cp[e], wdv[e], (1, 1))
        g, u = acts[e][:, :hid], acts[e][:, hid:]
        p = jnp.concatenate([w[e * chunk:(e + 1) * chunk] for w in weights], axis=0)
        s = 1.0 / (1.0 + jnp.exp(-g))
        silu = g * s
        hidden = (silu * u).astype(BF).astype(F32)
        prods.append(jnp.sum(hidden * q, axis=1, keepdims=True))
        dh = p * q
        hp[e, :, :hid] = (p * hidden).astype(BF)
        hp[e, :, hid:2 * hid] = (dh * u * s * (1.0 + g * (1.0 - s))).astype(BF)
        hp[e, :, 2 * hid:] = (dh * silu).astype(BF)
    begin(hp, hs, sem_o.at[2], o_copies)
    for e in range(local):
        out = dot(hp[e, :, :hid], wdv[e], (1, 0)).astype(BF)
        for k in range(pairs):
            row[k, pl.ds(e * chunk, chunk), :] = out[k * chunk:(k + 1) * chunk]
    for k in range(pairs):
        for y, at in enumerate((mine, theirs)):
            part = dot(picks[k], row[k, :, pl.ds(at, half)], (1, 0)).astype(BF)
            for b in range(2):
                (outk, outs)[k % 2][(y * 2 + b) * count + k // 2] = part[b * rows:(b + 1) * rows]
    for k in range(2):
        half_out = pl.ds(0, 4 * count)
        begin((outk, outs)[k].at[half_out], (keep, send)[k].at[half_out], sem_o.at[3 + k], o_copies)
    for e in range(local):
        out = dot(hp[e, :, hid:], wgu[e], (1, 1)).astype(BF)
        for k in range(pairs):
            row[k, pl.ds(e * chunk, chunk), :] = out[k * chunk:(k + 1) * chunk]
    for k in (*range(1, pairs, 2), *range(0, pairs, 2)):
        for y, at in enumerate((mine, theirs)):
            part = dot(picks[k], row[k, :, pl.ds(at, half)], (1, 0)).astype(BF)
            for b in range(2):
                (outk, outs)[k % 2][(4 + b * 2 + y) * count + k // 2] = part[b * rows:(b + 1) * rows]
        for b in range(4):
            slot = (4 + b) * count + k // 2
            begin((outk, outs)[k % 2].at[slot], (keep, send)[k % 2].at[slot], sem_o.at[5 + 4 * k + b], o_copies)
    for k in range(pairs):
        prod = jnp.concatenate([v[k * chunk:(k + 1) * chunk] for v in prods], axis=0)
        high = prod.astype(BF).astype(F32)
        spread = (jnp.where(s_lane == s_row // chunk, high, 0.0)
                  + jnp.where(s_lane == s_row // chunk + wide // 2, prod - high, 0.0)).astype(BF)
        both = dot(picks[k], spread, (1, 0)).T
        gp[:, pl.ds(k * two, two)] = both[:8] + both[wide // 2:wide // 2 + 8]
    for copy in o_copies:
        copy.wait()


def rounds(at, pieces, cap, wg, wu, wd):
    count = len(pieces) // 8
    rows = pieces[0].shape[0]
    local, width, hid = wg.shape
    half = width // 2
    n = count * 4 * rows
    wide = pieces[0].shape[1] - width - half
    packed = count * 4 * cap
    anyspec = pl.BlockSpec(memory_space=pl.ANY)
    vspec = pl.BlockSpec(memory_space=pltpu.VMEM)
    return pl.pallas_call(
        functools.partial(rounds_kernel, cap, count),
        in_specs=[pl.BlockSpec(memory_space=pltpu.SMEM)] + [anyspec] * (8 * count + 3),
        out_specs=[anyspec] * 5 + [vspec],
        out_shape=[
            jax.ShapeDtypeStruct((local, packed, width), BF),
            jax.ShapeDtypeStruct((local, packed, width), BF),
            jax.ShapeDtypeStruct((local, packed, 3 * hid), BF),
            jax.ShapeDtypeStruct((8 * count, rows, half), BF),
            jax.ShapeDtypeStruct((8 * count, rows, half), BF),
            jax.ShapeDtypeStruct((8, n), F32),
        ],
        scratch_shapes=[
            pltpu.VMEM((8 * count, rows, half), BF),
            pltpu.VMEM((8 * count, rows, half), BF),
            pltpu.VMEM((n, wide), BF),
            pltpu.VMEM((local, width, 2 * hid), BF),
            pltpu.VMEM((local, hid, width), BF),
            pltpu.VMEM((local, packed, width), BF),
            pltpu.VMEM((local, packed, width), BF),
            pltpu.VMEM((local, packed, 3 * hid), BF),
            pltpu.VMEM((2 * count, local * 2 * cap, width), BF),
            pltpu.SemaphoreType.DMA((8 * count,)),
            pltpu.SemaphoreType.DMA((8 * count,)),
            pltpu.SemaphoreType.DMA((4 * count,)),
            pltpu.SemaphoreType.DMA((3 * local,)),
            pltpu.SemaphoreType.DMA((5 + 8 * count,)),
        ],
        compiler_params=pltpu.CompilerParams(vmem_limit_bytes=44 * 1024 * 1024),
        cost_estimate=pl.CostEstimate(
            flops=12 * local * packed * width * hid, bytes_accessed=2 * (3 * local * hid * width + 6 * n * width),
            transcendentals=local * packed * hid),
        name="moe_rounds",
    )(at, *pieces, wg, wu, wd)


def weight_kernel(rounds, off, outs_n, *refs):
    acts, hs = refs[:rounds], refs[rounds:2 * rounds]
    outs = refs[2 * rounds:2 * rounds + outs_n]
    a, h = refs[2 * rounds + outs_n:2 * rounds + outs_n + 2]
    stage = refs[2 * rounds + outs_n + 2:2 * rounds + 2 * outs_n + 2]
    sem_a, sem_h, sem_o = refs[2 * rounds + 2 * outs_n + 2:]
    local, total, width = a.shape
    packed = total // rounds
    cols = h.shape[2]
    hid = cols // outs_n
    copies, o_copies = [], []
    for e in range(local):
        mine = []
        for r in range(rounds):
            begin(hs[r].at[e, :, pl.ds(off, cols)], h.at[e, pl.ds(r * packed, packed), :], sem_h.at[e, r], mine)
            begin(acts[r].at[e], a.at[e, pl.ds(r * packed, packed), :], sem_a.at[e, r], mine)
        copies.append(mine)
    step = 512
    for e in range(local):
        for copy in copies[e]:
            copy.wait()
        for j in range(width // step):
            block = pl.ds(j * step, step)
            if outs_n == 2:
                grad = dot(a[e, :, block], h[e], (0, 0)).astype(BF)
                for i in range(outs_n):
                    stage[i][e, block, :] = grad[:, i * hid:(i + 1) * hid]
                    begin(stage[i].at[e, block], outs[i].at[e, block], sem_o.at[e, j, i], o_copies)
            else:
                stage[0][e, :, block] = dot(h[e], a[e, :, block], (0, 0)).astype(BF)
                begin(stage[0].at[e, :, block], outs[0].at[e, :, block], sem_o.at[e, j, 0], o_copies)
    for copy in o_copies:
        copy.wait()


def weight_grads(acts, hs, off, cols, outs_n, shape, name):
    local, packed, width = acts[0].shape
    rounds = len(acts)
    anyspec = pl.BlockSpec(memory_space=pl.ANY)
    return pl.pallas_call(
        functools.partial(weight_kernel, rounds, off, outs_n),
        in_specs=[anyspec] * (2 * rounds),
        out_specs=[anyspec] * outs_n,
        out_shape=[jax.ShapeDtypeStruct(shape, BF)] * outs_n,
        scratch_shapes=[
            pltpu.VMEM((local, rounds * packed, width), BF),
            pltpu.VMEM((local, rounds * packed, cols), BF),
            *[pltpu.VMEM(shape, BF)] * outs_n,
            pltpu.SemaphoreType.DMA((local, rounds)),
            pltpu.SemaphoreType.DMA((local, rounds)),
            pltpu.SemaphoreType.DMA((local, width // 512, outs_n)),
        ],
        compiler_params=pltpu.CompilerParams(vmem_limit_bytes=22 * 1024 * 1024),
        cost_estimate=pl.CostEstimate(
            flops=2 * local * rounds * packed * width * cols,
            bytes_accessed=2 * local * (rounds * packed * (width + cols) + width * cols), transcendentals=0),
        name=name,
    )(*acts, *hs)


def dense_probs(routes, probs, experts):
    onehot = routes[:, :, None] == jnp.arange(experts, dtype=jnp.int32)
    return jnp.sum(jnp.where(onehot, probs[:, :, None], 0.0), axis=1), onehot


def add(*terms):
    return functools.reduce(lambda a, b: a + b, [t.astype(F32) for t in terms])


sync = lax.optimization_barrier


def add16(*terms):
    return add(*terms).astype(BF)


def body16(tokens, routes, probs, w_gate, w_up, w_down, cotangent):
    rows, width = tokens.shape
    half = width // 2
    local, _, hid = w_gate.shape
    owners = lax.axis_size("dp")
    experts = local * owners
    place = lax.axis_index("dp")
    col = lax.axis_index("col")
    z = place // 4
    middle = (z == 1) | (z == 2)

    def permute(pairs):
        return lambda v: lax.ppermute(v, "dp", pairs)

    over_core = permute([(i, i ^ 1) for i in range(16)])
    over_x = permute([(i, i ^ 2) for i in range(16)])
    over_z = permute([(i, i ^ 4) for i in range(16)])
    across = permute([(4 + j, 8 + j) for j in range(4)] + [(8 + j, 4 + j) for j in range(4)])
    outward = permute([(4 + j, j) for j in range(4)] + [(8 + j, 12 + j) for j in range(4)])
    leap = permute([(4 * a + j, 4 * b + j) for a, b in ((0, 1), (3, 2), (1, 3), (2, 0)) for j in range(4)])
    end_to_end = permute([(j, 12 + j) for j in range(4)] + [(12 + j, j) for j in range(4)])

    def over_y(v):
        return lax.ppermute(v, "col", [(0, 1), (1, 0)])

    table, onehot = dense_probs(routes, probs, experts)
    high = table.astype(BF)
    low = (table - high.astype(F32)).astype(BF)
    gap = jnp.zeros((rows, 64 - experts), BF)
    first = jnp.concatenate([tokens, cotangent, high, gap, low, gap], axis=1)

    def pair(own, other):
        return jnp.stack([own[:, width:width + half], other[:, width:width + half]])

    cap = 3 * rows * routes.shape[1] // (2 * experts)
    at = jnp.stack([col, place * local]).astype(jnp.int32)

    def run(*pieces):
        return rounds(at, pieces, cap, w_gate, w_up, w_down)

    def stage_one(keep, got):
        return over_y(add16(keep[4:8], got[4:8])), over_x(add16(keep[12:16], got[12:16]))

    def stage_two(keep, got, m_got, g_got):
        return (over_x(add16(keep[2:4], got[2:4], m_got[2:4])),
                over_y(add16(keep[10:12], got[10:12], g_got[2:4])))

    def layer_sum(keep, got, one, two, r):
        return jnp.stack([add(keep[r], got[r], one[0][r], two[0][r]),
                          add(keep[8 + r], got[8 + r], one[1][r], two[1][r])])

    l0 = first
    l1, b1, x0 = over_z(l0), across(l0), over_x(l0)
    l0, l1, b1, x0 = sync((l0, l1, b1, x0))

    c1, b2, x1, y0 = across(l1), outward(b1), over_x(l1), over_y(pair(l0, x0))
    k0, kx0 = over_core(l0), over_core(x0)
    l0, l1, b1, b2, c1, x0, x1, y0 = sync((l0, l1, b1, b2, c1, x0, x1, y0))

    l2 = jnp.where(middle, c1, b2)
    c2, x2, y1 = outward(c1), over_x(l2), over_y(pair(l1, x1))
    k1, kx1, ky0 = over_core(l1), over_core(x1), over_core(y0)
    l2, c2, x2, y1 = sync((l2, c2, x2, y1))

    l3 = jnp.where(middle, b1, c2)
    x3, y2, y3 = over_x(l3), over_y(pair(l2, x2)), over_y(l3[None, :, width:width + half])
    ky1 = over_core(y1)
    k2, kx2, k3 = over_core(l2), over_core(x2), over_core(l3)
    xs_a, cs_a, hs_a, keep_a, send_a, gp_a = run(
        l0, x0, k0, kx0, y0, y0, ky0, ky0, l1, x1, k1, kx1, y1, y1, ky1, ky1)
    l2, x2, l3, x3, y2, y3, k2, kx2, k3, keep_a, send_a = sync(
        (l2, x2, l3, x3, y2, y3, k2, kx2, k3, keep_a, send_a))

    yx3 = over_y(x3[None, :, width:width + half])
    ky2, kx3, ky3 = over_core(y2), over_core(x3), over_core(y3)
    got_a = over_core(send_a)
    yx3, ky2, kx3, ky3, keep_a, got_a = sync((yx3, ky2, kx3, ky3, keep_a, got_a))

    kyx3 = over_core(yx3)
    one_a = stage_one(keep_a, got_a)
    xs_b, cs_b, hs_b, keep_b, send_b, gp_b = run(
        l2, x2, k2, kx2, y2, y2, ky2, ky2, l3, x3, k3, kx3, y3, yx3, ky3, kyx3)
    one_a, keep_b, send_b = sync((one_a, keep_b, send_b))

    got_b = over_core(send_b)
    two_a = stage_two(keep_a, got_a, *one_a)
    got_b, two_a = sync((got_b, two_a))

    one_b = stage_one(keep_b, got_b)
    from1 = over_z(layer_sum(keep_a, got_a, one_a, two_a, 1).astype(BF))
    grad_gate, grad_up = weight_grads([xs_a, xs_b], [hs_a, hs_b], hid, 2 * hid, 2, w_gate.shape, "grad_in")
    gps = jnp.concatenate([gp_a[:local], gp_b[:local]], axis=1).reshape(local, 4, 4, rows)
    gps = gps[:, :, jnp.array([0, 2, 1, 3])].reshape(local, owners, rows).transpose(1, 0, 2)
    gps = gps[jnp.arange(owners) ^ place]
    one_b, from1, grad_gate, grad_up, gps = sync((one_b, from1, grad_gate, grad_up, gps))

    two_b = stage_two(keep_b, got_b, *one_b)
    back = lax.all_to_all(gps, "dp", 0, 0, tiled=True)
    two_b, back = sync((two_b, back))

    sum2, sum3 = layer_sum(keep_b, got_b, one_b, two_b, 0).astype(BF), layer_sum(keep_b, got_b, one_b, two_b, 1)
    step, ends = leap(sum2), end_to_end(sum3.astype(BF))
    (grad_down,) = weight_grads([cs_a, cs_b], [hs_a, hs_b], 0, hid, 1, w_down.shape, "grad_down")
    other_back = over_y(back)
    sum3, step, ends, grad_down, other_back = sync((sum3, step, ends, grad_down, other_back))

    inner = across(add16(sum3, step))
    result = add16(layer_sum(keep_a, got_a, one_a, two_a, 0), from1, jnp.where(middle, inner, add16(step, ends)))

    back = (back + other_back).reshape(experts, rows).T
    grad_probs = jnp.sum(jnp.where(onehot, back[:, None, :], 0.0), axis=2)
    return result[0], result[1], grad_probs, grad_gate, grad_up, grad_down


def body_any(tokens, routes, probs, w_gate, w_up, w_down, cotangent):
    rows, width = tokens.shape
    half = width // 2
    local, _, hid = w_gate.shape
    owners = lax.axis_size("dp")
    experts = local * owners
    parts = max(1, rows * owners // 2048)
    step = rows // parts
    table, onehot = dense_probs(routes, probs, experts)
    arrived = lax.all_to_all(table.reshape(rows, owners, local).transpose(1, 0, 2), "dp", 0, 0, tiled=True)
    def one_part(grads, inputs):
        own_x, own_c, own_p = inputs
        x = lax.all_gather(own_x, "dp", axis=0, tiled=True)
        c = lax.all_gather(lax.all_gather(own_c, "dp", axis=0, tiled=True), "col", axis=1, tiled=True)
        p = own_p.reshape(owners * step, local).T[:, :, None]
        gate = jnp.einsum("td,ldh->lth", x, w_gate, preferred_element_type=F32)
        up = jnp.einsum("td,ldh->lth", x, w_up, preferred_element_type=F32)
        q = jnp.einsum("td,lhd->lth", c, w_down, preferred_element_type=F32)
        s = jax.nn.sigmoid(gate)
        silu = gate * s
        hidden = (silu * up).astype(BF).astype(F32)
        dh = p * q
        hp = (p * hidden).astype(BF)
        dg = (dh * up * s * (1.0 + gate * (1.0 - s))).astype(BF)
        du = (dh * silu).astype(BF)
        m = jnp.einsum("lth,lhd->td", hp, w_down, preferred_element_type=F32).astype(BF)
        g = (jnp.einsum("lth,ldh->td", dg, w_gate, preferred_element_type=F32)
             + jnp.einsum("lth,ldh->td", du, w_up, preferred_element_type=F32)).astype(BF)
        sums = []
        for part in (m, g):
            part = lax.psum_scatter(part, "dp", scatter_dimension=0, tiled=True)
            sums.append(lax.psum_scatter(part, "col", scatter_dimension=1, tiled=True))
        new = (jnp.einsum("td,lth->ldh", x, dg, preferred_element_type=F32),
               jnp.einsum("td,lth->ldh", x, du, preferred_element_type=F32),
               jnp.einsum("lth,td->lhd", hp, c, preferred_element_type=F32))
        grads = tuple(a + b for a, b in zip(grads, new))
        return grads, (*sums, jnp.sum(hidden * q, axis=2))

    zeros = tuple(jnp.zeros(w.shape, F32) for w in (w_gate, w_up, w_down))
    arrived = arrived.reshape(owners, parts, step, local).transpose(1, 0, 2, 3)
    grads, (mixed, grad_tokens, gps) = lax.scan(
        one_part, zeros,
        (tokens.reshape(parts, step, width), cotangent.reshape(parts, step, half), arrived))
    back = gps.reshape(parts, local, owners, step).transpose(2, 0, 3, 1).reshape(owners, rows, local)
    back = lax.all_to_all(back, "dp", 0, 0, tiled=True)
    back = lax.psum(back.transpose(1, 0, 2).reshape(rows, experts), "col")
    grad_probs = jnp.sum(jnp.where(onehot, back[:, None, :], 0.0), axis=2)
    return (mixed.reshape(rows, half), grad_tokens.reshape(rows, half), grad_probs,
            *(v.astype(BF) for v in grads))


def solution(mesh):
    body = body16 if mesh.shape["dp"] == 16 and mesh.shape["col"] == 2 else body_any
    return jax.shard_map(
        body,
        mesh=mesh,
        in_specs=(
            P("dp", None),
            P("dp", None),
            P("dp", None),
            P("dp", None, "col"),
            P("dp", None, "col"),
            P("dp", "col", None),
            P("dp", "col"),
        ),
        out_specs=(
            P("dp", "col"),
            P("dp", "col"),
            P("dp", None),
            P("dp", None, "col"),
            P("dp", None, "col"),
            P("dp", "col", None),
        ),
        check_vma=False,
    )
```

```python
import functools

import jax
import jax.numpy as jnp
from jax import lax
from jax.experimental import pallas as pl
from jax.experimental.pallas import tpu as pltpu
from jax.sharding import PartitionSpec as P

BF = jnp.bfloat16
F32 = jnp.float32


def dot(a, b, dims):
    return lax.dot_general(a, b, ((dims[:1], dims[1:]), ((), ())), preferred_element_type=F32)


def begin(src, dst, sem, into):
    copy = pltpu.make_async_copy(src, dst, sem)
    copy.start()
    into.append(copy)


def rounds_kernel(cap, count, index, at_ref, *refs):
    views = [ref if i is None else ref.at[i] for ref, i in zip(refs, index)]
    groups = [views[8 * i:8 * i + 8] for i in range(count)]
    blocks = [group[b] for group in groups for b in range(4)]
    others = [group[4 + b] for group in groups for b in range(4)]
    (wg, wu, wd, xs, cs, hs, keep, send, gp,
     x, c, tab, wgu, wdv, xp, cp, hp, row,
     sem_x, sem_c, sem_t, sem_w, sem_o) = refs[8 * count:]
    rows = blocks[0].shape[0]
    pairs = 2 * count
    local, width, hid = wg.shape
    half = width // 2
    outk, outs = x, c
    wide = tab.shape[1]
    col = at_ref[0]
    first = at_ref[1]
    mine = pl.multiple_of(col * half, half)
    theirs = pl.multiple_of((1 - col) * half, half)
    held = 4 * count
    x_copies, c_copies, t_copies, w_copies, o_copies = [], [], [], [], []

    for b, piece in enumerate(blocks):
        begin(piece.at[:, pl.ds(width + half, wide)], tab.at[pl.ds(b * rows, rows), :], sem_t.at[b], t_copies)
    for b, piece in enumerate(blocks):
        for y in range(2):
            begin(piece.at[:, pl.ds(y * half, half)], x.at[y * held + b], sem_x.at[y * held + b], x_copies)
    for e in range(local):
        begin(wg.at[e], wgu.at[e, :, pl.ds(0, hid)], sem_w.at[3 * e], w_copies)
        begin(wu.at[e], wgu.at[e, :, pl.ds(hid, hid)], sem_w.at[3 * e + 1], w_copies)
    for b, piece in enumerate(blocks):
        begin(piece.at[:, pl.ds(width, half)], c.at[col * held + b], sem_c.at[b], c_copies)
        begin(others[b], c.at[(1 - col) * held + b], sem_c.at[held + b], c_copies)
    for e in range(local):
        begin(wd.at[e], wdv.at[e], sem_w.at[3 * e + 2], w_copies)

    two = 2 * rows
    chunk = 2 * cap
    slots = local * chunk
    r_id = lax.broadcasted_iota(jnp.int32, (two, two), 0)
    c_id = lax.broadcasted_iota(jnp.int32, (two, two), 1)
    lower = ((c_id < r_id) & ((c_id < rows) == (r_id < rows))).astype(BF)
    lane = lax.broadcasted_iota(jnp.int32, (two, wide), 1)
    slot_id = lax.broadcasted_iota(jnp.int32, (two, slots), 1)
    base = jnp.where(lax.broadcasted_iota(jnp.int32, (two, 1), 0) < rows, 0, cap)
    s_lane = lax.broadcasted_iota(jnp.int32, (slots, wide), 1)
    s_row = lax.broadcasted_iota(jnp.int32, (slots, wide), 0)
    s_expert = first + s_row // chunk
    for copy in t_copies:
        copy.wait()
    picks, weights = [], []
    for k in range(pairs):
        values = tab[pl.ds(k * two, two), :]
        routed = values.astype(F32) > 0
        before = dot(lower, jnp.where(routed, 1.0, 0.0).astype(BF), (1, 0))
        pick = jnp.zeros((two, slots), F32)
        for e in range(local):
            here = (lane == first + e) & routed
            rank = jnp.sum(jnp.where(here, before + 1.0, 0.0), axis=1, keepdims=True).astype(jnp.int32)
            target = jnp.where(rank > 0, rank - 1 + e * chunk + base, -1)
            pick = pick + jnp.where(slot_id == target, 1.0, 0.0)
        pick = pick.astype(BF)
        picked = dot(pick, values, (0, 0))
        chosen = (s_lane == s_expert) | (s_lane == s_expert + wide // 2)
        picks.append(pick)
        weights.append(jnp.sum(jnp.where(chosen, picked, 0.0), axis=1, keepdims=True))

    def gather(src, dst):
        for k in range(pairs):
            for y in range(2):
                part = dot(picks[k], src[pl.ds(y * held + 2 * k, 2)].reshape(two, half), (0, 0)).astype(BF)
                for e in range(local):
                    dst[e, pl.ds(k * chunk, chunk), pl.ds(y * half, half)] = part[e * chunk:(e + 1) * chunk]

    for copy in x_copies:
        copy.wait()
    gather(x, xp)
    begin(xp, xs, sem_o.at[0], o_copies)
    acts = []
    for e in range(local):
        w_copies[2 * e].wait()
        w_copies[2 * e + 1].wait()
        acts.append(dot(xp[e], wgu[e], (1, 0)))
    for copy in c_copies:
        copy.wait()
    gather(c, cp)
    begin(cp, cs, sem_o.at[1], o_copies)
    prods = []
    for e in range(local):
        w_copies[2 * local + e].wait()
        q = dot(cp[e], wdv[e], (1, 1))
        g, u = acts[e][:, :hid], acts[e][:, hid:]
        p = jnp.concatenate([w[e * chunk:(e + 1) * chunk] for w in weights], axis=0)
        s = 1.0 / (1.0 + jnp.exp(-g))
        silu = g * s
        hidden = (silu * u).astype(BF).astype(F32)
        prods.append(jnp.sum(hidden * q, axis=1, keepdims=True))
        dh = p * q
        hp[e, :, :hid] = (p * hidden).astype(BF)
        hp[e, :, hid:2 * hid] = (dh * u * s * (1.0 + g * (1.0 - s))).astype(BF)
        hp[e, :, 2 * hid:] = (dh * silu).astype(BF)
    begin(hp, hs, sem_o.at[2], o_copies)
    for e in range(local):
        out = dot(hp[e, :, :hid], wdv[e], (1, 0)).astype(BF)
        for k in range(pairs):
            row[k, pl.ds(e * chunk, chunk), :] = out[k * chunk:(k + 1) * chunk]
    for k in range(pairs):
        for y, at in enumerate((mine, theirs)):
            part = dot(picks[k], row[k, :, pl.ds(at, half)], (1, 0)).astype(BF)
            for b in range(2):
                (outk, outs)[k % 2][(y * 2 + b) * count + k // 2] = part[b * rows:(b + 1) * rows]
    for k in range(2):
        half_out = pl.ds(0, 4 * count)
        begin((outk, outs)[k].at[half_out], (keep, send)[k].at[half_out], sem_o.at[3 + k], o_copies)
    for e in range(local):
        out = dot(hp[e, :, hid:], wgu[e], (1, 1)).astype(BF)
        for k in range(pairs):
            row[k, pl.ds(e * chunk, chunk), :] = out[k * chunk:(k + 1) * chunk]
    for k in (*range(1, pairs, 2), *range(0, pairs, 2)):
        for y, at in enumerate((mine, theirs)):
            part = dot(picks[k], row[k, :, pl.ds(at, half)], (1, 0)).astype(BF)
            for b in range(2):
                (outk, outs)[k % 2][(4 + b * 2 + y) * count + k // 2] = part[b * rows:(b + 1) * rows]
        for b in range(4):
            slot = (4 + b) * count + k // 2
            begin((outk, outs)[k % 2].at[slot], (keep, send)[k % 2].at[slot], sem_o.at[5 + 4 * k + b], o_copies)
    for k in range(pairs):
        prod = jnp.concatenate([v[k * chunk:(k + 1) * chunk] for v in prods], axis=0)
        high = prod.astype(BF).astype(F32)
        spread = (jnp.where(s_lane == s_row // chunk, high, 0.0)
                  + jnp.where(s_lane == s_row // chunk + wide // 2, prod - high, 0.0)).astype(BF)
        both = dot(picks[k], spread, (1, 0)).T
        gp[:, pl.ds(k * two, two)] = both[:8] + both[wide // 2:wide // 2 + 8]
    for copy in o_copies:
        copy.wait()


def rounds(at, pieces, cap, wg, wu, wd):
    count = len(pieces) // 8
    pieces, index = zip(*(p if isinstance(p, tuple) else (p, None) for p in pieces))
    rows = pieces[0].shape[0]
    local, width, hid = wg.shape
    half = width // 2
    n = count * 4 * rows
    wide = pieces[0].shape[1] - width - half
    packed = count * 4 * cap
    anyspec = pl.BlockSpec(memory_space=pl.ANY)
    vspec = pl.BlockSpec(memory_space=pltpu.VMEM)
    return pl.pallas_call(
        functools.partial(rounds_kernel, cap, count, index),
        in_specs=[pl.BlockSpec(memory_space=pltpu.SMEM)] + [anyspec] * (8 * count + 3),
        out_specs=[anyspec] * 5 + [vspec],
        out_shape=[
            jax.ShapeDtypeStruct((local, packed, width), BF),
            jax.ShapeDtypeStruct((local, packed, width), BF),
            jax.ShapeDtypeStruct((local, packed, 3 * hid), BF),
            jax.ShapeDtypeStruct((8 * count, rows, half), BF),
            jax.ShapeDtypeStruct((8 * count, rows, half), BF),
            jax.ShapeDtypeStruct((8, n), F32),
        ],
        scratch_shapes=[
            pltpu.VMEM((8 * count, rows, half), BF),
            pltpu.VMEM((8 * count, rows, half), BF),
            pltpu.VMEM((n, wide), BF),
            pltpu.VMEM((local, width, 2 * hid), BF),
            pltpu.VMEM((local, hid, width), BF),
            pltpu.VMEM((local, packed, width), BF),
            pltpu.VMEM((local, packed, width), BF),
            pltpu.VMEM((local, packed, 3 * hid), BF),
            pltpu.VMEM((2 * count, local * 2 * cap, width), BF),
            pltpu.SemaphoreType.DMA((8 * count,)),
            pltpu.SemaphoreType.DMA((8 * count,)),
            pltpu.SemaphoreType.DMA((4 * count,)),
            pltpu.SemaphoreType.DMA((3 * local,)),
            pltpu.SemaphoreType.DMA((5 + 8 * count,)),
        ],
        compiler_params=pltpu.CompilerParams(vmem_limit_bytes=44 * 1024 * 1024),
        cost_estimate=pl.CostEstimate(
            flops=12 * local * packed * width * hid, bytes_accessed=2 * (3 * local * hid * width + 6 * n * width),
            transcendentals=local * packed * hid),
        name="moe_rounds",
    )(at, *pieces, wg, wu, wd)


def weight_kernel(rounds, off, outs_n, *refs):
    acts, hs = refs[:rounds], refs[rounds:2 * rounds]
    outs = refs[2 * rounds:2 * rounds + outs_n]
    a, h = refs[2 * rounds + outs_n:2 * rounds + outs_n + 2]
    stage = refs[2 * rounds + outs_n + 2:2 * rounds + 2 * outs_n + 2]
    sem_a, sem_h, sem_o = refs[2 * rounds + 2 * outs_n + 2:]
    local, total, width = a.shape
    packed = total // rounds
    cols = h.shape[2]
    hid = cols // outs_n
    copies, o_copies = [], []
    for e in range(local):
        mine = []
        for r in range(rounds):
            begin(hs[r].at[e, :, pl.ds(off, cols)], h.at[e, pl.ds(r * packed, packed), :], sem_h.at[e, r], mine)
            begin(acts[r].at[e], a.at[e, pl.ds(r * packed, packed), :], sem_a.at[e, r], mine)
        copies.append(mine)
    step = 512
    for e in range(local):
        for copy in copies[e]:
            copy.wait()
        for j in range(width // step):
            block = pl.ds(j * step, step)
            if outs_n == 2:
                grad = dot(a[e, :, block], h[e], (0, 0)).astype(BF)
                for i in range(outs_n):
                    stage[i][e, block, :] = grad[:, i * hid:(i + 1) * hid]
                    begin(stage[i].at[e, block], outs[i].at[e, block], sem_o.at[e, j, i], o_copies)
            else:
                stage[0][e, :, block] = dot(h[e], a[e, :, block], (0, 0)).astype(BF)
                begin(stage[0].at[e, :, block], outs[0].at[e, :, block], sem_o.at[e, j, 0], o_copies)
    for copy in o_copies:
        copy.wait()


def weight_grads(acts, hs, off, cols, outs_n, shape, name):
    local, packed, width = acts[0].shape
    rounds = len(acts)
    anyspec = pl.BlockSpec(memory_space=pl.ANY)
    return pl.pallas_call(
        functools.partial(weight_kernel, rounds, off, outs_n),
        in_specs=[anyspec] * (2 * rounds),
        out_specs=[anyspec] * outs_n,
        out_shape=[jax.ShapeDtypeStruct(shape, BF)] * outs_n,
        scratch_shapes=[
            pltpu.VMEM((local, rounds * packed, width), BF),
            pltpu.VMEM((local, rounds * packed, cols), BF),
            *[pltpu.VMEM(shape, BF)] * outs_n,
            pltpu.SemaphoreType.DMA((local, rounds)),
            pltpu.SemaphoreType.DMA((local, rounds)),
            pltpu.SemaphoreType.DMA((local, width // 512, outs_n)),
        ],
        compiler_params=pltpu.CompilerParams(vmem_limit_bytes=22 * 1024 * 1024),
        cost_estimate=pl.CostEstimate(
            flops=2 * local * rounds * packed * width * cols,
            bytes_accessed=2 * local * (rounds * packed * (width + cols) + width * cols), transcendentals=0),
        name=name,
    )(*acts, *hs)


def dense_probs(routes, probs, experts):
    onehot = routes[:, :, None] == jnp.arange(experts, dtype=jnp.int32)
    return jnp.sum(jnp.where(onehot, probs[:, :, None], 0.0), axis=1), onehot


def add(*terms):
    return functools.reduce(lambda a, b: a + b, [t.astype(F32) for t in terms])


sync = lax.optimization_barrier


def add16(*terms):
    return add(*terms).astype(BF)


def body16(tokens, routes, probs, w_gate, w_up, w_down, cotangent):
    rows, width = tokens.shape
    half = width // 2
    local, _, hid = w_gate.shape
    owners = lax.axis_size("dp")
    experts = local * owners
    place = lax.axis_index("dp")
    col = lax.axis_index("col")
    z = place // 4
    middle = (z == 1) | (z == 2)

    def permute(pairs):
        return lambda v: lax.ppermute(v, "dp", pairs)

    over_core = permute([(i, i ^ 1) for i in range(16)])
    over_x = permute([(i, i ^ 2) for i in range(16)])
    over_z = permute([(i, i ^ 4) for i in range(16)])
    across = permute([(4 + j, 8 + j) for j in range(4)] + [(8 + j, 4 + j) for j in range(4)])
    outward = permute([(4 + j, j) for j in range(4)] + [(8 + j, 12 + j) for j in range(4)])
    leap = permute([(4 * a + j, 4 * b + j) for a, b in ((0, 1), (3, 2), (1, 3), (2, 0)) for j in range(4)])
    end_to_end = permute([(j, 12 + j) for j in range(4)] + [(12 + j, j) for j in range(4)])

    def over_y(v):
        return lax.ppermute(v, "col", [(0, 1), (1, 0)])

    table, onehot = dense_probs(routes, probs, experts)
    high = table.astype(BF)
    low = (table - high.astype(F32)).astype(BF)
    gap = jnp.zeros((rows, 64 - experts), BF)
    first = jnp.concatenate([tokens, cotangent, high, gap, low, gap], axis=1)

    def cotangents(*sources):
        return jnp.stack([v[:, width:width + half] for v in sources])

    cap = 3 * rows * routes.shape[1] // (2 * experts)
    at = jnp.stack([col, place * local]).astype(jnp.int32)

    def run(*pieces):
        return rounds(at, pieces, cap, w_gate, w_up, w_down)

    def stage_one(keep, got):
        return over_y(add16(keep[4:8], got[4:8])), over_x(add16(keep[12:16], got[12:16]))

    def stage_two(keep, got, m_got, g_got):
        return (over_x(add16(keep[2:4], got[2:4], m_got[2:4])),
                over_y(add16(keep[10:12], got[10:12], g_got[2:4])))

    def layer_sum(keep, got, one, two, r):
        return jnp.stack([add(keep[r], got[r], one[0][r], two[0][r]),
                          add(keep[8 + r], got[8 + r], one[1][r], two[1][r])])

    l0 = first
    l1, b1, x0 = over_z(l0), across(l0), over_x(l0)
    l0, l1, b1, x0 = sync((l0, l1, b1, x0))

    c1, b2, x1, y0 = across(l1), outward(b1), over_x(l1), over_y(cotangents(l0, x0))
    k0, kx0 = over_core(l0), over_core(x0)
    l0, l1, b1, b2, c1, x0, x1, y0 = sync((l0, l1, b1, b2, c1, x0, x1, y0))

    l2 = jnp.where(middle, c1, b2)
    c2, x2, y1 = outward(c1), over_x(l2), over_y(cotangents(l1, x1))
    k1, kx1, ky0 = over_core(l1), over_core(x1), over_core(y0)
    l2, c2, x2, y1 = sync((l2, c2, x2, y1))

    l3 = jnp.where(middle, b1, c2)
    x3, y2 = over_x(l3), over_y(cotangents(l2, x2, l3))
    ky1 = over_core(y1)
    k2, kx2, k3 = over_core(l2), over_core(x2), over_core(l3)
    xs_a, cs_a, hs_a, keep_a, send_a, gp_a = run(
        l0, x0, k0, kx0, (y0, 0), (y0, 1), (ky0, 0), (ky0, 1),
        l1, x1, k1, kx1, (y1, 0), (y1, 1), (ky1, 0), (ky1, 1))
    l2, x2, l3, x3, y2, k2, kx2, k3, keep_a, send_a = sync(
        (l2, x2, l3, x3, y2, k2, kx2, k3, keep_a, send_a))

    yx3, ky2, kx3 = over_y(cotangents(x3)), over_core(y2), over_core(x3)
    got_a = over_core(send_a)
    yx3, ky2, kx3, keep_a, got_a = sync((yx3, ky2, kx3, keep_a, got_a))

    kyx3 = over_core(yx3)
    one_a = stage_one(keep_a, got_a)
    xs_b, cs_b, hs_b, keep_b, send_b, gp_b = run(
        l2, x2, k2, kx2, (y2, 0), (y2, 1), (ky2, 0), (ky2, 1),
        l3, x3, k3, kx3, (y2, 2), (yx3, 0), (ky2, 2), (kyx3, 0))
    one_a, keep_b, send_b = sync((one_a, keep_b, send_b))

    got_b = over_core(send_b)
    two_a = stage_two(keep_a, got_a, *one_a)
    got_b, two_a = sync((got_b, two_a))

    def first_sums(i):
        return over_y(add16(keep_b[4 + i:8:2], got_b[4 + i:8:2])), over_x(add16(keep_b[12 + i:16:2], got_b[12 + i:16:2]))

    def second_sums(i, one):
        return (over_x(add16(keep_b[2 + i], got_b[2 + i], one[0][1])),
                over_y(add16(keep_b[10 + i], got_b[10 + i], one[1][1])))

    def whole_sum(i, one, two):
        return jnp.stack([add16(keep_b[i], got_b[i], one[0][0], two[0]),
                          add16(keep_b[8 + i], got_b[8 + i], one[1][0], two[1])])

    one_2 = first_sums(0)
    gps = jnp.concatenate([gp_a[:local], gp_b[:local]], axis=1).reshape(local, 4, 4, rows)
    gps = gps[:, :, jnp.array([0, 2, 1, 3])].reshape(local, owners, rows).transpose(1, 0, 2)
    gps = gps[jnp.arange(owners) ^ place]
    one_2, gps = sync((one_2, gps))

    one_3, two_2 = first_sums(1), second_sums(0, one_2)
    from1 = over_z(layer_sum(keep_a, got_a, one_a, two_a, 1).astype(BF))
    grad_gate, grad_up = weight_grads([xs_a, xs_b], [hs_a, hs_b], hid, 2 * hid, 2, w_gate.shape, "grad_in")
    one_3, two_2, from1, grad_gate, grad_up = sync((one_3, two_2, from1, grad_gate, grad_up))

    two_3 = second_sums(1, one_3)
    step = leap(whole_sum(0, one_2, two_2))
    back = lax.all_to_all(gps, "dp", 0, 0, tiled=True)
    two_3, step, back = sync((two_3, step, back))

    sum3 = whole_sum(1, one_3, two_3)
    ends, inner = end_to_end(sum3), across(add16(sum3, step))
    other_back = over_y(back)
    (grad_down,) = weight_grads([cs_a, cs_b], [hs_a, hs_b], 0, hid, 1, w_down.shape, "grad_down")
    ends, inner, other_back, grad_down = sync((ends, inner, other_back, grad_down))
    own = layer_sum(keep_a, got_a, one_a, two_a, 0)
    result = add16(own, from1, jnp.where(middle, inner, add16(step, ends)))

    back = (back + other_back).reshape(experts, rows).T
    grad_probs = jnp.sum(jnp.where(onehot, back[:, None, :], 0.0), axis=2)
    return result[0], result[1], grad_probs, grad_gate, grad_up, grad_down


def body_any(tokens, routes, probs, w_gate, w_up, w_down, cotangent):
    rows, width = tokens.shape
    half = width // 2
    local, _, hid = w_gate.shape
    owners = lax.axis_size("dp")
    experts = local * owners
    parts = max(1, rows * owners // 2048)
    step = rows // parts
    table, onehot = dense_probs(routes, probs, experts)
    arrived = lax.all_to_all(table.reshape(rows, owners, local).transpose(1, 0, 2), "dp", 0, 0, tiled=True)
    def one_part(grads, inputs):
        own_x, own_c, own_p = inputs
        x = lax.all_gather(own_x, "dp", axis=0, tiled=True)
        c = lax.all_gather(lax.all_gather(own_c, "dp", axis=0, tiled=True), "col", axis=1, tiled=True)
        p = own_p.reshape(owners * step, local).T[:, :, None]
        gate = jnp.einsum("td,ldh->lth", x, w_gate, preferred_element_type=F32)
        up = jnp.einsum("td,ldh->lth", x, w_up, preferred_element_type=F32)
        q = jnp.einsum("td,lhd->lth", c, w_down, preferred_element_type=F32)
        s = jax.nn.sigmoid(gate)
        silu = gate * s
        hidden = (silu * up).astype(BF).astype(F32)
        dh = p * q
        hp = (p * hidden).astype(BF)
        dg = (dh * up * s * (1.0 + gate * (1.0 - s))).astype(BF)
        du = (dh * silu).astype(BF)
        m = jnp.einsum("lth,lhd->td", hp, w_down, preferred_element_type=F32).astype(BF)
        g = (jnp.einsum("lth,ldh->td", dg, w_gate, preferred_element_type=F32)
             + jnp.einsum("lth,ldh->td", du, w_up, preferred_element_type=F32)).astype(BF)
        sums = []
        for part in (m, g):
            part = lax.psum_scatter(part, "dp", scatter_dimension=0, tiled=True)
            sums.append(lax.psum_scatter(part, "col", scatter_dimension=1, tiled=True))
        new = (jnp.einsum("td,lth->ldh", x, dg, preferred_element_type=F32),
               jnp.einsum("td,lth->ldh", x, du, preferred_element_type=F32),
               jnp.einsum("lth,td->lhd", hp, c, preferred_element_type=F32))
        grads = tuple(a + b for a, b in zip(grads, new))
        return grads, (*sums, jnp.sum(hidden * q, axis=2))

    zeros = tuple(jnp.zeros(w.shape, F32) for w in (w_gate, w_up, w_down))
    arrived = arrived.reshape(owners, parts, step, local).transpose(1, 0, 2, 3)
    grads, (mixed, grad_tokens, gps) = lax.scan(
        one_part, zeros,
        (tokens.reshape(parts, step, width), cotangent.reshape(parts, step, half), arrived))
    back = gps.reshape(parts, local, owners, step).transpose(2, 0, 3, 1).reshape(owners, rows, local)
    back = lax.all_to_all(back, "dp", 0, 0, tiled=True)
    back = lax.psum(back.transpose(1, 0, 2).reshape(rows, experts), "col")
    grad_probs = jnp.sum(jnp.where(onehot, back[:, None, :], 0.0), axis=2)
    return (mixed.reshape(rows, half), grad_tokens.reshape(rows, half), grad_probs,
            *(v.astype(BF) for v in grads))


def solution(mesh):
    body = body16 if mesh.shape["dp"] == 16 and mesh.shape["col"] == 2 else body_any
    return jax.shard_map(
        body,
        mesh=mesh,
        in_specs=(
            P("dp", None),
            P("dp", None),
            P("dp", None),
            P("dp", None, "col"),
            P("dp", None, "col"),
            P("dp", "col", None),
            P("dp", "col"),
        ),
        out_specs=(
            P("dp", "col"),
            P("dp", "col"),
            P("dp", None),
            P("dp", None, "col"),
            P("dp", None, "col"),
            P("dp", "col", None),
        ),
        check_vma=False,
    )
```

```python
import functools

import jax
import jax.numpy as jnp
from jax import lax
from jax.experimental import pallas as pl
from jax.experimental.pallas import tpu as pltpu
from jax.sharding import PartitionSpec as P

BF = jnp.bfloat16
F32 = jnp.float32


def dot(a, b, dims):
    return lax.dot_general(a, b, ((dims[:1], dims[1:]), ((), ())), preferred_element_type=F32)


def begin(src, dst, sem, into):
    copy = pltpu.make_async_copy(src, dst, sem)
    copy.start()
    into.append(copy)


def rounds_kernel(cap, count, index, split, at_ref, *refs):
    views = [ref if i is None else ref.at[i] for ref, i in zip(refs, index)]
    groups = [views[8 * i:8 * i + 8] for i in range(count)]
    blocks = [group[b] for group in groups for b in range(4)]
    others = [group[4 + b] for group in groups for b in range(4)]
    wg, wu, wd, xs, cs, hs, gp = refs[8 * count:8 * count + 7]
    split_n = count if split else 1
    results = [refs[8 * count + 7 + k * split_n:8 * count + 7 + (k + 1) * split_n] for k in range(2)]
    (x, c, tab, wgu, wdv, xp, cp, hp, row,
     sem_x, sem_c, sem_t, sem_w, sem_o) = refs[8 * count + 7 + 2 * split_n:]

    def slot(i, layer):
        return layer * 8 + i if split else i * count + layer

    rows = blocks[0].shape[0]
    pairs = 2 * count
    local, width, hid = wg.shape
    half = width // 2
    outk, outs = x, c
    wide = tab.shape[1]
    col = at_ref[0]
    first = at_ref[1]
    mine = pl.multiple_of(col * half, half)
    theirs = pl.multiple_of((1 - col) * half, half)
    held = 4 * count
    x_copies, c_copies, t_copies, w_copies, o_copies = [], [], [], [], []

    for b, piece in enumerate(blocks):
        begin(piece.at[:, pl.ds(width + half, wide)], tab.at[pl.ds(b * rows, rows), :], sem_t.at[b], t_copies)
    for b, piece in enumerate(blocks):
        for y in range(2):
            begin(piece.at[:, pl.ds(y * half, half)], x.at[y * held + b], sem_x.at[y * held + b], x_copies)
    for e in range(local):
        begin(wg.at[e], wgu.at[e, :, pl.ds(0, hid)], sem_w.at[3 * e], w_copies)
        begin(wu.at[e], wgu.at[e, :, pl.ds(hid, hid)], sem_w.at[3 * e + 1], w_copies)
    for b, piece in enumerate(blocks):
        begin(piece.at[:, pl.ds(width, half)], c.at[col * held + b], sem_c.at[b], c_copies)
        begin(others[b], c.at[(1 - col) * held + b], sem_c.at[held + b], c_copies)
    for e in range(local):
        begin(wd.at[e], wdv.at[e], sem_w.at[3 * e + 2], w_copies)

    two = 2 * rows
    chunk = 2 * cap
    slots = local * chunk
    r_id = lax.broadcasted_iota(jnp.int32, (two, two), 0)
    c_id = lax.broadcasted_iota(jnp.int32, (two, two), 1)
    lower = ((c_id < r_id) & ((c_id < rows) == (r_id < rows))).astype(BF)
    lane = lax.broadcasted_iota(jnp.int32, (two, wide), 1)
    slot_id = lax.broadcasted_iota(jnp.int32, (two, slots), 1)
    base = jnp.where(lax.broadcasted_iota(jnp.int32, (two, 1), 0) < rows, 0, cap)
    s_lane = lax.broadcasted_iota(jnp.int32, (slots, wide), 1)
    s_row = lax.broadcasted_iota(jnp.int32, (slots, wide), 0)
    s_expert = first + s_row // chunk
    for copy in t_copies:
        copy.wait()
    picks, weights = [], []
    for k in range(pairs):
        values = tab[pl.ds(k * two, two), :]
        routed = values.astype(F32) > 0
        before = dot(lower, jnp.where(routed, 1.0, 0.0).astype(BF), (1, 0))
        pick = jnp.zeros((two, slots), F32)
        for e in range(local):
            here = (lane == first + e) & routed
            rank = jnp.sum(jnp.where(here, before + 1.0, 0.0), axis=1, keepdims=True).astype(jnp.int32)
            target = jnp.where(rank > 0, rank - 1 + e * chunk + base, -1)
            pick = pick + jnp.where(slot_id == target, 1.0, 0.0)
        pick = pick.astype(BF)
        picked = dot(pick, values, (0, 0))
        chosen = (s_lane == s_expert) | (s_lane == s_expert + wide // 2)
        picks.append(pick)
        weights.append(jnp.sum(jnp.where(chosen, picked, 0.0), axis=1, keepdims=True))

    def gather(src, dst):
        for k in range(pairs):
            for y in range(2):
                part = dot(picks[k], src[pl.ds(y * held + 2 * k, 2)].reshape(two, half), (0, 0)).astype(BF)
                for e in range(local):
                    dst[e, pl.ds(k * chunk, chunk), pl.ds(y * half, half)] = part[e * chunk:(e + 1) * chunk]

    for copy in x_copies:
        copy.wait()
    gather(x, xp)
    begin(xp, xs, sem_o.at[0], o_copies)
    acts = []
    for e in range(local):
        w_copies[2 * e].wait()
        w_copies[2 * e + 1].wait()
        acts.append(dot(xp[e], wgu[e], (1, 0)))
    for copy in c_copies:
        copy.wait()
    gather(c, cp)
    begin(cp, cs, sem_o.at[1], o_copies)
    prods = []
    for e in range(local):
        w_copies[2 * local + e].wait()
        q = dot(cp[e], wdv[e], (1, 1))
        g, u = acts[e][:, :hid], acts[e][:, hid:]
        p = jnp.concatenate([w[e * chunk:(e + 1) * chunk] for w in weights], axis=0)
        s = 1.0 / (1.0 + jnp.exp(-g))
        silu = g * s
        hidden = (silu * u).astype(BF).astype(F32)
        prods.append(jnp.sum(hidden * q, axis=1, keepdims=True))
        dh = p * q
        hp[e, :, :hid] = (p * hidden).astype(BF)
        hp[e, :, hid:2 * hid] = (dh * u * s * (1.0 + g * (1.0 - s))).astype(BF)
        hp[e, :, 2 * hid:] = (dh * silu).astype(BF)
    begin(hp, hs, sem_o.at[2], o_copies)
    for e in range(local):
        out = dot(hp[e, :, :hid], wdv[e], (1, 0)).astype(BF)
        for k in range(pairs):
            row[k, pl.ds(e * chunk, chunk), :] = out[k * chunk:(k + 1) * chunk]
    for k in range(pairs):
        for y, at in enumerate((mine, theirs)):
            part = dot(picks[k], row[k, :, pl.ds(at, half)], (1, 0)).astype(BF)
            for b in range(2):
                (outk, outs)[k % 2][slot(y * 2 + b, k // 2)] = part[b * rows:(b + 1) * rows]
    for k in range(2):
        for r in range(split_n):
            size = 4 * count // split_n
            begin((outk, outs)[k].at[pl.ds(r * 8, size)], results[k][r].at[pl.ds(0, size)],
                  sem_o.at[3 + 2 * k + r], o_copies)
    for e in range(local):
        out = dot(hp[e, :, hid:], wgu[e], (1, 1)).astype(BF)
        for k in range(pairs):
            row[k, pl.ds(e * chunk, chunk), :] = out[k * chunk:(k + 1) * chunk]
    for k in (*range(1, pairs, 2), *range(0, pairs, 2)):
        for y, at in enumerate((mine, theirs)):
            part = dot(picks[k], row[k, :, pl.ds(at, half)], (1, 0)).astype(BF)
            for b in range(2):
                (outk, outs)[k % 2][slot(4 + b * 2 + y, k // 2)] = part[b * rows:(b + 1) * rows]
        for b in range(4):
            held_at = slot(4 + b, k // 2)
            into = results[k % 2][k // 2].at[4 + b] if split else results[k % 2][0].at[held_at]
            begin((outk, outs)[k % 2].at[held_at], into, sem_o.at[7 + 4 * k + b], o_copies)
    for k in range(pairs):
        prod = jnp.concatenate([v[k * chunk:(k + 1) * chunk] for v in prods], axis=0)
        high = prod.astype(BF).astype(F32)
        spread = (jnp.where(s_lane == s_row // chunk, high, 0.0)
                  + jnp.where(s_lane == s_row // chunk + wide // 2, prod - high, 0.0)).astype(BF)
        both = dot(picks[k], spread, (1, 0)).T
        gp[:, pl.ds(k * two, two)] = both[:8] + both[wide // 2:wide // 2 + 8]
    for copy in o_copies:
        copy.wait()


def rounds(at, pieces, cap, wg, wu, wd, split):
    count = len(pieces) // 8
    pieces, index = zip(*(p if isinstance(p, tuple) else (p, None) for p in pieces))
    rows = pieces[0].shape[0]
    local, width, hid = wg.shape
    half = width // 2
    n = count * 4 * rows
    wide = pieces[0].shape[1] - width - half
    packed = count * 4 * cap
    each = 8 if split else 8 * count
    results = [jax.ShapeDtypeStruct((each, rows, half), BF)] * (16 * count // each)
    anyspec = pl.BlockSpec(memory_space=pl.ANY)
    vspec = pl.BlockSpec(memory_space=pltpu.VMEM)
    return pl.pallas_call(
        functools.partial(rounds_kernel, cap, count, index, split),
        in_specs=[pl.BlockSpec(memory_space=pltpu.SMEM)] + [anyspec] * (8 * count + 3),
        out_specs=[anyspec] * 3 + [vspec] + [anyspec] * len(results),
        out_shape=[
            jax.ShapeDtypeStruct((local, packed, width), BF),
            jax.ShapeDtypeStruct((local, packed, width), BF),
            jax.ShapeDtypeStruct((local, packed, 3 * hid), BF),
            jax.ShapeDtypeStruct((8, n), F32),
            *results,
        ],
        scratch_shapes=[
            pltpu.VMEM((8 * count, rows, half), BF),
            pltpu.VMEM((8 * count, rows, half), BF),
            pltpu.VMEM((n, wide), BF),
            pltpu.VMEM((local, width, 2 * hid), BF),
            pltpu.VMEM((local, hid, width), BF),
            pltpu.VMEM((local, packed, width), BF),
            pltpu.VMEM((local, packed, width), BF),
            pltpu.VMEM((local, packed, 3 * hid), BF),
            pltpu.VMEM((2 * count, local * 2 * cap, width), BF),
            pltpu.SemaphoreType.DMA((8 * count,)),
            pltpu.SemaphoreType.DMA((8 * count,)),
            pltpu.SemaphoreType.DMA((4 * count,)),
            pltpu.SemaphoreType.DMA((3 * local,)),
            pltpu.SemaphoreType.DMA((7 + 8 * count,)),
        ],
        compiler_params=pltpu.CompilerParams(vmem_limit_bytes=44 * 1024 * 1024),
        cost_estimate=pl.CostEstimate(
            flops=12 * local * packed * width * hid, bytes_accessed=2 * (3 * local * hid * width + 6 * n * width),
            transcendentals=local * packed * hid),
        name="moe_rounds",
    )(at, *pieces, wg, wu, wd)


def weight_kernel(rounds, off, outs_n, *refs):
    acts, hs = refs[:rounds], refs[rounds:2 * rounds]
    outs = refs[2 * rounds:2 * rounds + outs_n]
    a, h = refs[2 * rounds + outs_n:2 * rounds + outs_n + 2]
    stage = refs[2 * rounds + outs_n + 2:2 * rounds + 2 * outs_n + 2]
    sem_a, sem_h, sem_o = refs[2 * rounds + 2 * outs_n + 2:]
    local, total, width = a.shape
    packed = total // rounds
    cols = h.shape[2]
    hid = cols // outs_n
    copies, o_copies = [], []
    for e in range(local):
        mine = []
        for r in range(rounds):
            begin(hs[r].at[e, :, pl.ds(off, cols)], h.at[e, pl.ds(r * packed, packed), :], sem_h.at[e, r], mine)
            begin(acts[r].at[e], a.at[e, pl.ds(r * packed, packed), :], sem_a.at[e, r], mine)
        copies.append(mine)
    step = 512
    for e in range(local):
        for copy in copies[e]:
            copy.wait()
        for j in range(width // step):
            block = pl.ds(j * step, step)
            if outs_n == 2:
                grad = dot(a[e, :, block], h[e], (0, 0)).astype(BF)
                for i in range(outs_n):
                    stage[i][e, block, :] = grad[:, i * hid:(i + 1) * hid]
                    begin(stage[i].at[e, block], outs[i].at[e, block], sem_o.at[e, j, i], o_copies)
            else:
                stage[0][e, :, block] = dot(h[e], a[e, :, block], (0, 0)).astype(BF)
                begin(stage[0].at[e, :, block], outs[0].at[e, :, block], sem_o.at[e, j, 0], o_copies)
    for copy in o_copies:
        copy.wait()


def weight_grads(acts, hs, off, cols, outs_n, shape, name):
    local, packed, width = acts[0].shape
    rounds = len(acts)
    anyspec = pl.BlockSpec(memory_space=pl.ANY)
    return pl.pallas_call(
        functools.partial(weight_kernel, rounds, off, outs_n),
        in_specs=[anyspec] * (2 * rounds),
        out_specs=[anyspec] * outs_n,
        out_shape=[jax.ShapeDtypeStruct(shape, BF)] * outs_n,
        scratch_shapes=[
            pltpu.VMEM((local, rounds * packed, width), BF),
            pltpu.VMEM((local, rounds * packed, cols), BF),
            *[pltpu.VMEM(shape, BF)] * outs_n,
            pltpu.SemaphoreType.DMA((local, rounds)),
            pltpu.SemaphoreType.DMA((local, rounds)),
            pltpu.SemaphoreType.DMA((local, width // 512, outs_n)),
        ],
        compiler_params=pltpu.CompilerParams(vmem_limit_bytes=22 * 1024 * 1024),
        cost_estimate=pl.CostEstimate(
            flops=2 * local * rounds * packed * width * cols,
            bytes_accessed=2 * local * (rounds * packed * (width + cols) + width * cols), transcendentals=0),
        name=name,
    )(*acts, *hs)


def dense_probs(routes, probs, experts):
    onehot = routes[:, :, None] == jnp.arange(experts, dtype=jnp.int32)
    return jnp.sum(jnp.where(onehot, probs[:, :, None], 0.0), axis=1), onehot


def add(*terms):
    return functools.reduce(lambda a, b: a + b, [t.astype(F32) for t in terms])


sync = lax.optimization_barrier


def add16(*terms):
    return add(*terms).astype(BF)


def body16(tokens, routes, probs, w_gate, w_up, w_down, cotangent):
    rows, width = tokens.shape
    half = width // 2
    local, _, hid = w_gate.shape
    owners = lax.axis_size("dp")
    experts = local * owners
    place = lax.axis_index("dp")
    col = lax.axis_index("col")
    z = place // 4
    middle = (z == 1) | (z == 2)

    def permute(pairs):
        return lambda v: lax.ppermute(v, "dp", pairs)

    over_core = permute([(i, i ^ 1) for i in range(16)])
    over_x = permute([(i, i ^ 2) for i in range(16)])
    over_z = permute([(i, i ^ 4) for i in range(16)])
    across = permute([(4 + j, 8 + j) for j in range(4)] + [(8 + j, 4 + j) for j in range(4)])
    outward = permute([(4 + j, j) for j in range(4)] + [(8 + j, 12 + j) for j in range(4)])
    leap = permute([(4 * a + j, 4 * b + j) for a, b in ((0, 1), (3, 2), (1, 3), (2, 0)) for j in range(4)])
    end_to_end = permute([(j, 12 + j) for j in range(4)] + [(12 + j, j) for j in range(4)])

    def over_y(v):
        return lax.ppermute(v, "col", [(0, 1), (1, 0)])

    table, onehot = dense_probs(routes, probs, experts)
    high = table.astype(BF)
    low = (table - high.astype(F32)).astype(BF)
    gap = jnp.zeros((rows, 64 - experts), BF)
    first = jnp.concatenate([tokens, cotangent, high, gap, low, gap], axis=1)

    def cotangents(*sources):
        return jnp.stack([v[:, width:width + half] for v in sources])

    cap = 3 * rows * routes.shape[1] // (2 * experts)
    at = jnp.stack([col, place * local]).astype(jnp.int32)

    def run(*pieces, split=False):
        return rounds(at, pieces, cap, w_gate, w_up, w_down, split)

    def stage_one(keep, got):
        return over_y(add16(keep[4:8], got[4:8])), over_x(add16(keep[12:16], got[12:16]))

    def stage_two(keep, got, m_got, g_got):
        return (over_x(add16(keep[2:4], got[2:4], m_got[2:4])),
                over_y(add16(keep[10:12], got[10:12], g_got[2:4])))

    def layer_sum(keep, got, one, two, r):
        return jnp.stack([add(keep[r], got[r], one[0][r], two[0][r]),
                          add(keep[8 + r], got[8 + r], one[1][r], two[1][r])])

    l0 = first
    l1, b1, x0 = over_z(l0), across(l0), over_x(l0)
    l0, l1, b1, x0 = sync((l0, l1, b1, x0))

    c1, b2, x1, y0 = across(l1), outward(b1), over_x(l1), over_y(cotangents(l0, x0))
    k0, kx0 = over_core(l0), over_core(x0)
    l0, l1, b1, b2, c1, x0, x1, y0 = sync((l0, l1, b1, b2, c1, x0, x1, y0))

    l2 = jnp.where(middle, c1, b2)
    c2, x2, y1 = outward(c1), over_x(l2), over_y(cotangents(l1, x1))
    k1, kx1, ky0 = over_core(l1), over_core(x1), over_core(y0)
    l2, c2, x2, y1 = sync((l2, c2, x2, y1))

    l3 = jnp.where(middle, b1, c2)
    x3, y2 = over_x(l3), over_y(cotangents(l2, x2, l3))
    ky1 = over_core(y1)
    k2, kx2, k3 = over_core(l2), over_core(x2), over_core(l3)
    xs_a, cs_a, hs_a, gp_a, keep_a, send_a = run(
        l0, x0, k0, kx0, (y0, 0), (y0, 1), (ky0, 0), (ky0, 1),
        l1, x1, k1, kx1, (y1, 0), (y1, 1), (ky1, 0), (ky1, 1))
    l2, x2, l3, x3, y2, k2, kx2, k3, keep_a, send_a = sync(
        (l2, x2, l3, x3, y2, k2, kx2, k3, keep_a, send_a))

    yx3, ky2, kx3 = over_y(cotangents(x3)), over_core(y2), over_core(x3)
    got_a = over_core(send_a)
    yx3, ky2, kx3, keep_a, got_a = sync((yx3, ky2, kx3, keep_a, got_a))

    kyx3 = over_core(yx3)
    one_a = stage_one(keep_a, got_a)
    xs_b, cs_b, hs_b, gp_b, keep2, keep3, send2, send3 = run(
        l2, x2, k2, kx2, (y2, 0), (y2, 1), (ky2, 0), (ky2, 1),
        l3, x3, k3, kx3, (y2, 2), (yx3, 0), (ky2, 2), (kyx3, 0), split=True)
    one_a, keep2, keep3, send2, send3 = sync((one_a, keep2, keep3, send2, send3))

    got2, got3 = over_core(send2), over_core(send3)
    two_a = stage_two(keep_a, got_a, *one_a)
    got2, keep2 = sync((got2, keep2))

    def first_sums(keep, got):
        return over_y(add16(keep[2:4], got[2:4])), over_x(add16(keep[6:8], got[6:8]))

    def second_sums(keep, got, one):
        return over_x(add16(keep[1], got[1], one[0][1])), over_y(add16(keep[5], got[5], one[1][1]))

    def whole_sum(keep, got, one, two):
        return jnp.stack([add16(keep[0], got[0], one[0][0], two[0]), add16(keep[4], got[4], one[1][0], two[1])])

    one_2 = first_sums(keep2, got2)
    gps = jnp.concatenate([gp_a[:local], gp_b[:local]], axis=1).reshape(local, 4, 4, rows)
    gps = gps[:, :, jnp.array([0, 2, 1, 3])].reshape(local, owners, rows).transpose(1, 0, 2)
    gps = gps[jnp.arange(owners) ^ place]
    one_2, two_a, gps = sync((one_2, two_a, gps))

    one_3, two_2 = first_sums(keep3, got3), second_sums(keep2, got2, one_2)
    from1 = over_z(layer_sum(keep_a, got_a, one_a, two_a, 1).astype(BF))
    grad_gate, grad_up = weight_grads([xs_a, xs_b], [hs_a, hs_b], hid, 2 * hid, 2, w_gate.shape, "grad_in")
    one_3, two_2, from1, grad_gate, grad_up = sync((one_3, two_2, from1, grad_gate, grad_up))

    two_3 = second_sums(keep3, got3, one_3)
    step = leap(whole_sum(keep2, got2, one_2, two_2))
    back = lax.all_to_all(gps, "dp", 0, 0, tiled=True)
    two_3, step, back = sync((two_3, step, back))

    sum3 = whole_sum(keep3, got3, one_3, two_3)
    ends, inner = end_to_end(sum3), across(add16(sum3, step))
    other_back = over_y(back)
    (grad_down,) = weight_grads([cs_a, cs_b], [hs_a, hs_b], 0, hid, 1, w_down.shape, "grad_down")
    ends, inner, other_back, grad_down = sync((ends, inner, other_back, grad_down))
    own = layer_sum(keep_a, got_a, one_a, two_a, 0)
    result = add16(own, from1, jnp.where(middle, inner, add16(step, ends)))

    back = (back + other_back).reshape(experts, rows).T
    grad_probs = jnp.sum(jnp.where(onehot, back[:, None, :], 0.0), axis=2)
    return result[0], result[1], grad_probs, grad_gate, grad_up, grad_down


def body_any(tokens, routes, probs, w_gate, w_up, w_down, cotangent):
    rows, width = tokens.shape
    half = width // 2
    local, _, hid = w_gate.shape
    owners = lax.axis_size("dp")
    experts = local * owners
    parts = max(1, rows * owners // 2048)
    step = rows // parts
    table, onehot = dense_probs(routes, probs, experts)
    arrived = lax.all_to_all(table.reshape(rows, owners, local).transpose(1, 0, 2), "dp", 0, 0, tiled=True)
    def one_part(grads, inputs):
        own_x, own_c, own_p = inputs
        x = lax.all_gather(own_x, "dp", axis=0, tiled=True)
        c = lax.all_gather(lax.all_gather(own_c, "dp", axis=0, tiled=True), "col", axis=1, tiled=True)
        p = own_p.reshape(owners * step, local).T[:, :, None]
        gate = jnp.einsum("td,ldh->lth", x, w_gate, preferred_element_type=F32)
        up = jnp.einsum("td,ldh->lth", x, w_up, preferred_element_type=F32)
        q = jnp.einsum("td,lhd->lth", c, w_down, preferred_element_type=F32)
        s = jax.nn.sigmoid(gate)
        silu = gate * s
        hidden = (silu * up).astype(BF).astype(F32)
        dh = p * q
        hp = (p * hidden).astype(BF)
        dg = (dh * up * s * (1.0 + gate * (1.0 - s))).astype(BF)
        du = (dh * silu).astype(BF)
        m = jnp.einsum("lth,lhd->td", hp, w_down, preferred_element_type=F32).astype(BF)
        g = (jnp.einsum("lth,ldh->td", dg, w_gate, preferred_element_type=F32)
             + jnp.einsum("lth,ldh->td", du, w_up, preferred_element_type=F32)).astype(BF)
        sums = []
        for part in (m, g):
            part = lax.psum_scatter(part, "dp", scatter_dimension=0, tiled=True)
            sums.append(lax.psum_scatter(part, "col", scatter_dimension=1, tiled=True))
        new = (jnp.einsum("td,lth->ldh", x, dg, preferred_element_type=F32),
               jnp.einsum("td,lth->ldh", x, du, preferred_element_type=F32),
               jnp.einsum("lth,td->lhd", hp, c, preferred_element_type=F32))
        grads = tuple(a + b for a, b in zip(grads, new))
        return grads, (*sums, jnp.sum(hidden * q, axis=2))

    zeros = tuple(jnp.zeros(w.shape, F32) for w in (w_gate, w_up, w_down))
    arrived = arrived.reshape(owners, parts, step, local).transpose(1, 0, 2, 3)
    grads, (mixed, grad_tokens, gps) = lax.scan(
        one_part, zeros,
        (tokens.reshape(parts, step, width), cotangent.reshape(parts, step, half), arrived))
    back = gps.reshape(parts, local, owners, step).transpose(2, 0, 3, 1).reshape(owners, rows, local)
    back = lax.all_to_all(back, "dp", 0, 0, tiled=True)
    back = lax.psum(back.transpose(1, 0, 2).reshape(rows, experts), "col")
    grad_probs = jnp.sum(jnp.where(onehot, back[:, None, :], 0.0), axis=2)
    return (mixed.reshape(rows, half), grad_tokens.reshape(rows, half), grad_probs,
            *(v.astype(BF) for v in grads))


def solution(mesh):
    body = body16 if mesh.shape["dp"] == 16 and mesh.shape["col"] == 2 else body_any
    return jax.shard_map(
        body,
        mesh=mesh,
        in_specs=(
            P("dp", None),
            P("dp", None),
            P("dp", None),
            P("dp", None, "col"),
            P("dp", None, "col"),
            P("dp", "col", None),
            P("dp", "col"),
        ),
        out_specs=(
            P("dp", "col"),
            P("dp", "col"),
            P("dp", None),
            P("dp", None, "col"),
            P("dp", None, "col"),
            P("dp", "col", None),
        ),
        check_vma=False,
    )
```

```python
import functools

import jax
import jax.numpy as jnp
from jax import lax
from jax.experimental import pallas as pl
from jax.experimental.pallas import tpu as pltpu
from jax.sharding import PartitionSpec as P

BF = jnp.bfloat16
F32 = jnp.float32


def dot(a, b, dims):
    return lax.dot_general(a, b, ((dims[:1], dims[1:]), ((), ())), preferred_element_type=F32)


def begin(src, dst, sem, into):
    copy = pltpu.make_async_copy(src, dst, sem)
    copy.start()
    into.append(copy)


def rounds_kernel(cap, count, index, split, at_ref, *refs):
    views = [ref if i is None else ref.at[i] for ref, i in zip(refs, index)]
    groups = [views[8 * i:8 * i + 8] for i in range(count)]
    blocks = [group[b] for group in groups for b in range(4)]
    others = [group[4 + b] for group in groups for b in range(4)]
    wg, wu, wd, xs, cs, hs, gp = refs[8 * count:8 * count + 7]
    split_n = count if split else 1
    results = [refs[8 * count + 7 + k * split_n:8 * count + 7 + (k + 1) * split_n] for k in range(2)]
    (x, c, tab, wgu, wdv, xp, cp, hp, row,
     sem_x, sem_c, sem_t, sem_w, sem_o) = refs[8 * count + 7 + 2 * split_n:]

    def slot(i, layer):
        return layer * 8 + i if split else i * count + layer

    rows = blocks[0].shape[0]
    pairs = 2 * count
    local, width, hid = wg.shape
    half = width // 2
    outk, outs = x, c
    wide = tab.shape[1]
    col = at_ref[0]
    first = at_ref[1]
    mine = pl.multiple_of(col * half, half)
    theirs = pl.multiple_of((1 - col) * half, half)
    held = 4 * count
    x_copies, c_copies, t_copies, w_copies, o_copies = [], [], [], [], []

    for b, piece in enumerate(blocks):
        begin(piece.at[:, pl.ds(width + half, wide)], tab.at[pl.ds(b * rows, rows), :], sem_t.at[b], t_copies)
    for b, piece in enumerate(blocks):
        for y in range(2):
            begin(piece.at[:, pl.ds(y * half, half)], x.at[y * held + b], sem_x.at[y * held + b], x_copies)
    for e in range(local):
        begin(wg.at[e], wgu.at[e, :, pl.ds(0, hid)], sem_w.at[3 * e], w_copies)
        begin(wu.at[e], wgu.at[e, :, pl.ds(hid, hid)], sem_w.at[3 * e + 1], w_copies)
    for b, piece in enumerate(blocks):
        begin(piece.at[:, pl.ds(width, half)], c.at[col * held + b], sem_c.at[b], c_copies)
        begin(others[b], c.at[(1 - col) * held + b], sem_c.at[held + b], c_copies)
    for e in range(local):
        begin(wd.at[e], wdv.at[e], sem_w.at[3 * e + 2], w_copies)

    two = 2 * rows
    chunk = 2 * cap
    slots = local * chunk
    r_id = lax.broadcasted_iota(jnp.int32, (two, two), 0)
    c_id = lax.broadcasted_iota(jnp.int32, (two, two), 1)
    lower = ((c_id < r_id) & ((c_id < rows) == (r_id < rows))).astype(BF)
    lane = lax.broadcasted_iota(jnp.int32, (two, wide), 1)
    slot_id = lax.broadcasted_iota(jnp.int32, (two, slots), 1)
    base = jnp.where(lax.broadcasted_iota(jnp.int32, (two, 1), 0) < rows, 0, cap)
    s_lane = lax.broadcasted_iota(jnp.int32, (slots, wide), 1)
    s_row = lax.broadcasted_iota(jnp.int32, (slots, wide), 0)
    s_expert = first + s_row // chunk
    for copy in t_copies:
        copy.wait()
    picks, weights = [], []
    for k in range(pairs):
        values = tab[pl.ds(k * two, two), :]
        routed = values.astype(F32) > 0
        before = dot(lower, jnp.where(routed, 1.0, 0.0).astype(BF), (1, 0))
        pick = jnp.zeros((two, slots), F32)
        for e in range(local):
            here = (lane == first + e) & routed
            rank = jnp.sum(jnp.where(here, before + 1.0, 0.0), axis=1, keepdims=True).astype(jnp.int32)
            target = jnp.where(rank > 0, rank - 1 + e * chunk + base, -1)
            pick = pick + jnp.where(slot_id == target, 1.0, 0.0)
        pick = pick.astype(BF)
        picked = dot(pick, values, (0, 0))
        chosen = (s_lane == s_expert) | (s_lane == s_expert + wide // 2)
        picks.append(pick)
        weights.append(jnp.sum(jnp.where(chosen, picked, 0.0), axis=1, keepdims=True))

    def gather(src, dst):
        for k in range(pairs):
            for y in range(2):
                part = dot(picks[k], src[pl.ds(y * held + 2 * k, 2)].reshape(two, half), (0, 0)).astype(BF)
                for e in range(local):
                    dst[e, pl.ds(k * chunk, chunk), pl.ds(y * half, half)] = part[e * chunk:(e + 1) * chunk]

    for copy in x_copies:
        copy.wait()
    gather(x, xp)
    begin(xp, xs, sem_o.at[0], o_copies)
    acts = []
    for e in range(local):
        w_copies[2 * e].wait()
        w_copies[2 * e + 1].wait()
        acts.append(dot(xp[e], wgu[e], (1, 0)))
    for copy in c_copies:
        copy.wait()
    gather(c, cp)
    begin(cp, cs, sem_o.at[1], o_copies)
    prods = []
    for e in range(local):
        w_copies[2 * local + e].wait()
        q = dot(cp[e], wdv[e], (1, 1))
        g, u = acts[e][:, :hid], acts[e][:, hid:]
        p = jnp.concatenate([w[e * chunk:(e + 1) * chunk] for w in weights], axis=0)
        s = 1.0 / (1.0 + jnp.exp(-g))
        silu = g * s
        hidden = (silu * u).astype(BF).astype(F32)
        prods.append(jnp.sum(hidden * q, axis=1, keepdims=True))
        dh = p * q
        hp[e, :, :hid] = (p * hidden).astype(BF)
        hp[e, :, hid:2 * hid] = (dh * u * s * (1.0 + g * (1.0 - s))).astype(BF)
        hp[e, :, 2 * hid:] = (dh * silu).astype(BF)
    begin(hp, hs, sem_o.at[2], o_copies)
    for e in range(local):
        out = dot(hp[e, :, :hid], wdv[e], (1, 0)).astype(BF)
        for k in range(pairs):
            row[k, pl.ds(e * chunk, chunk), :] = out[k * chunk:(k + 1) * chunk]
    for k in range(pairs):
        for y, at in enumerate((mine, theirs)):
            part = dot(picks[k], row[k, :, pl.ds(at, half)], (1, 0)).astype(BF)
            for b in range(2):
                (outk, outs)[k % 2][slot(y * 2 + b, k // 2)] = part[b * rows:(b + 1) * rows]
    for k in range(2):
        for r in range(split_n):
            size = 4 * count // split_n
            begin((outk, outs)[k].at[pl.ds(r * 8, size)], results[k][r].at[pl.ds(0, size)],
                  sem_o.at[3 + 2 * k + r], o_copies)
    for e in range(local):
        out = dot(hp[e, :, hid:], wgu[e], (1, 1)).astype(BF)
        for k in range(pairs):
            row[k, pl.ds(e * chunk, chunk), :] = out[k * chunk:(k + 1) * chunk]
    for k in (*range(1, pairs, 2), *range(0, pairs, 2)):
        for y, at in enumerate((mine, theirs)):
            part = dot(picks[k], row[k, :, pl.ds(at, half)], (1, 0)).astype(BF)
            for b in range(2):
                (outk, outs)[k % 2][slot(4 + b * 2 + y, k // 2)] = part[b * rows:(b + 1) * rows]
        for b in range(4):
            held_at = slot(4 + b, k // 2)
            into = results[k % 2][k // 2].at[4 + b] if split else results[k % 2][0].at[held_at]
            begin((outk, outs)[k % 2].at[held_at], into, sem_o.at[7 + 4 * k + b], o_copies)
    for k in range(pairs):
        prod = jnp.concatenate([v[k * chunk:(k + 1) * chunk] for v in prods], axis=0)
        high = prod.astype(BF).astype(F32)
        spread = (jnp.where(s_lane == s_row // chunk, high, 0.0)
                  + jnp.where(s_lane == s_row // chunk + wide // 2, prod - high, 0.0)).astype(BF)
        both = dot(picks[k], spread, (1, 0)).T
        gp[:, pl.ds(k * two, two)] = both[:8] + both[wide // 2:wide // 2 + 8]
    for copy in o_copies:
        copy.wait()


def rounds(at, pieces, cap, wg, wu, wd, split):
    count = len(pieces) // 8
    pieces, index = zip(*(p if isinstance(p, tuple) else (p, None) for p in pieces))
    rows = pieces[0].shape[0]
    local, width, hid = wg.shape
    half = width // 2
    n = count * 4 * rows
    wide = pieces[0].shape[1] - width - half
    packed = count * 4 * cap
    each = 8 if split else 8 * count
    results = [jax.ShapeDtypeStruct((each, rows, half), BF)] * (16 * count // each)
    anyspec = pl.BlockSpec(memory_space=pl.ANY)
    vspec = pl.BlockSpec(memory_space=pltpu.VMEM)
    return pl.pallas_call(
        functools.partial(rounds_kernel, cap, count, index, split),
        in_specs=[pl.BlockSpec(memory_space=pltpu.SMEM)] + [anyspec] * (8 * count + 3),
        out_specs=[anyspec] * 3 + [vspec] + [anyspec] * len(results),
        out_shape=[
            jax.ShapeDtypeStruct((local, packed, width), BF),
            jax.ShapeDtypeStruct((local, packed, width), BF),
            jax.ShapeDtypeStruct((local, packed, 3 * hid), BF),
            jax.ShapeDtypeStruct((8, n), F32),
            *results,
        ],
        scratch_shapes=[
            pltpu.VMEM((8 * count, rows, half), BF),
            pltpu.VMEM((8 * count, rows, half), BF),
            pltpu.VMEM((n, wide), BF),
            pltpu.VMEM((local, width, 2 * hid), BF),
            pltpu.VMEM((local, hid, width), BF),
            pltpu.VMEM((local, packed, width), BF),
            pltpu.VMEM((local, packed, width), BF),
            pltpu.VMEM((local, packed, 3 * hid), BF),
            pltpu.VMEM((2 * count, local * 2 * cap, width), BF),
            pltpu.SemaphoreType.DMA((8 * count,)),
            pltpu.SemaphoreType.DMA((8 * count,)),
            pltpu.SemaphoreType.DMA((4 * count,)),
            pltpu.SemaphoreType.DMA((3 * local,)),
            pltpu.SemaphoreType.DMA((7 + 8 * count,)),
        ],
        compiler_params=pltpu.CompilerParams(vmem_limit_bytes=44 * 1024 * 1024),
        cost_estimate=pl.CostEstimate(
            flops=12 * local * packed * width * hid, bytes_accessed=2 * (3 * local * hid * width + 6 * n * width),
            transcendentals=local * packed * hid),
        name="moe_rounds",
    )(at, *pieces, wg, wu, wd)


def weight_kernel(rounds, off, outs_n, *refs):
    acts, hs = refs[:rounds], refs[rounds:2 * rounds]
    outs = refs[2 * rounds:2 * rounds + outs_n]
    a, h = refs[2 * rounds + outs_n:2 * rounds + outs_n + 2]
    stage = refs[2 * rounds + outs_n + 2:2 * rounds + 2 * outs_n + 2]
    sem_a, sem_h, sem_o = refs[2 * rounds + 2 * outs_n + 2:]
    local, total, width = a.shape
    packed = total // rounds
    cols = h.shape[2]
    hid = cols // outs_n
    copies, o_copies = [], []
    for e in range(local):
        mine = []
        for r in range(rounds):
            begin(hs[r].at[e, :, pl.ds(off, cols)], h.at[e, pl.ds(r * packed, packed), :], sem_h.at[e, r], mine)
            begin(acts[r].at[e], a.at[e, pl.ds(r * packed, packed), :], sem_a.at[e, r], mine)
        copies.append(mine)
    step = 512
    for e in range(local):
        for copy in copies[e]:
            copy.wait()
        for j in range(width // step):
            block = pl.ds(j * step, step)
            if outs_n == 2:
                grad = dot(a[e, :, block], h[e], (0, 0)).astype(BF)
                for i in range(outs_n):
                    stage[i][e, block, :] = grad[:, i * hid:(i + 1) * hid]
                    begin(stage[i].at[e, block], outs[i].at[e, block], sem_o.at[e, j, i], o_copies)
            else:
                stage[0][e, :, block] = dot(h[e], a[e, :, block], (0, 0)).astype(BF)
                begin(stage[0].at[e, :, block], outs[0].at[e, :, block], sem_o.at[e, j, 0], o_copies)
    for copy in o_copies:
        copy.wait()


def weight_grads(acts, hs, off, cols, outs_n, shape, name):
    local, packed, width = acts[0].shape
    rounds = len(acts)
    anyspec = pl.BlockSpec(memory_space=pl.ANY)
    return pl.pallas_call(
        functools.partial(weight_kernel, rounds, off, outs_n),
        in_specs=[anyspec] * (2 * rounds),
        out_specs=[anyspec] * outs_n,
        out_shape=[jax.ShapeDtypeStruct(shape, BF)] * outs_n,
        scratch_shapes=[
            pltpu.VMEM((local, rounds * packed, width), BF),
            pltpu.VMEM((local, rounds * packed, cols), BF),
            *[pltpu.VMEM(shape, BF)] * outs_n,
            pltpu.SemaphoreType.DMA((local, rounds)),
            pltpu.SemaphoreType.DMA((local, rounds)),
            pltpu.SemaphoreType.DMA((local, width // 512, outs_n)),
        ],
        compiler_params=pltpu.CompilerParams(vmem_limit_bytes=22 * 1024 * 1024),
        cost_estimate=pl.CostEstimate(
            flops=2 * local * rounds * packed * width * cols,
            bytes_accessed=2 * local * (rounds * packed * (width + cols) + width * cols), transcendentals=0),
        name=name,
    )(*acts, *hs)


def dense_probs(routes, probs, experts):
    onehot = routes[:, :, None] == jnp.arange(experts, dtype=jnp.int32)
    return jnp.sum(jnp.where(onehot, probs[:, :, None], 0.0), axis=1), onehot


def add(*terms):
    return functools.reduce(lambda a, b: a + b, [t.astype(F32) for t in terms])


sync = lax.optimization_barrier


def add16(*terms):
    return add(*terms).astype(BF)


def body16(tokens, routes, probs, w_gate, w_up, w_down, cotangent):
    rows, width = tokens.shape
    half = width // 2
    local, _, hid = w_gate.shape
    owners = lax.axis_size("dp")
    experts = local * owners
    place = lax.axis_index("dp")
    col = lax.axis_index("col")
    z = place // 4
    middle = (z == 1) | (z == 2)

    def permute(pairs):
        return lambda v: lax.ppermute(v, "dp", pairs)

    over_core = permute([(i, i ^ 1) for i in range(16)])
    over_x = permute([(i, i ^ 2) for i in range(16)])
    over_z = permute([(i, i ^ 4) for i in range(16)])
    across = permute([(4 + j, 8 + j) for j in range(4)] + [(8 + j, 4 + j) for j in range(4)])
    outward = permute([(4 + j, j) for j in range(4)] + [(8 + j, 12 + j) for j in range(4)])
    leap = permute([(4 * a + j, 4 * b + j) for a, b in ((0, 1), (3, 2), (1, 3), (2, 0)) for j in range(4)])
    end_to_end = permute([(j, 12 + j) for j in range(4)] + [(12 + j, j) for j in range(4)])

    def over_y(v):
        return lax.ppermute(v, "col", [(0, 1), (1, 0)])

    table, onehot = dense_probs(routes, probs, experts)
    high = table.astype(BF)
    low = (table - high.astype(F32)).astype(BF)
    gap = jnp.zeros((rows, 64 - experts), BF)
    first = jnp.concatenate([tokens, cotangent, high, gap, low, gap], axis=1)

    def cotangents(*sources):
        return jnp.stack([v[:, width:width + half] for v in sources])

    cap = 3 * rows * routes.shape[1] // (2 * experts)
    at = jnp.stack([col, place * local]).astype(jnp.int32)

    def run(*pieces, split=False):
        return rounds(at, pieces, cap, w_gate, w_up, w_down, split)

    def stage_one(keep, got):
        return over_y(add16(keep[4:8], got[4:8])), over_x(add16(keep[12:16], got[12:16]))

    def stage_two(keep, got, m_got, g_got):
        return (over_x(add16(keep[2:4], got[2:4], m_got[2:4])),
                over_y(add16(keep[10:12], got[10:12], g_got[2:4])))

    def layer_sum(keep, got, one, two, r):
        return jnp.stack([add(keep[r], got[r], one[0][r], two[0][r]),
                          add(keep[8 + r], got[8 + r], one[1][r], two[1][r])])

    l0 = first
    l1, b1, x0 = over_z(l0), across(l0), over_x(l0)
    l0, l1, b1, x0 = sync((l0, l1, b1, x0))

    c1, b2, x1, y0 = across(l1), outward(b1), over_x(l1), over_y(cotangents(l0, x0))
    k0, kx0 = over_core(l0), over_core(x0)
    l0, l1, b1, b2, c1, x0, x1, y0 = sync((l0, l1, b1, b2, c1, x0, x1, y0))

    l2 = jnp.where(middle, c1, b2)
    c2, x2, y1 = outward(c1), over_x(l2), over_y(cotangents(l1, x1))
    k1, kx1, ky0 = over_core(l1), over_core(x1), over_core(y0)
    l2, c2, x2, y1 = sync((l2, c2, x2, y1))

    l3 = jnp.where(middle, b1, c2)
    x3, y2 = over_x(l3), over_y(cotangents(l2, x2, l3))
    ky1 = over_core(y1)
    k2, kx2, k3 = over_core(l2), over_core(x2), over_core(l3)
    xs_a, cs_a, hs_a, gp_a, keep_a, send_a = run(
        l0, x0, k0, kx0, (y0, 0), (y0, 1), (ky0, 0), (ky0, 1),
        l1, x1, k1, kx1, (y1, 0), (y1, 1), (ky1, 0), (ky1, 1))
    l2, x2, l3, x3, y2, k2, kx2, k3, keep_a, send_a = sync(
        (l2, x2, l3, x3, y2, k2, kx2, k3, keep_a, send_a))

    yx3, ky2, kx3 = over_y(cotangents(x3)), over_core(y2), over_core(x3)
    got_a = over_core(send_a)
    yx3, ky2, kx3, keep_a, got_a = sync((yx3, ky2, kx3, keep_a, got_a))

    kyx3 = over_core(yx3)
    one_a = stage_one(keep_a, got_a)
    xs_b, cs_b, hs_b, gp_b, keep2, keep3, send2, send3 = run(
        l2, x2, k2, kx2, (y2, 0), (y2, 1), (ky2, 0), (ky2, 1),
        l3, x3, k3, kx3, (y2, 2), (yx3, 0), (ky2, 2), (kyx3, 0), split=True)
    one_a, keep2, keep3, send2, send3 = sync((one_a, keep2, keep3, send2, send3))

    got2, got3 = over_core(send2), over_core(send3)
    two_a = stage_two(keep_a, got_a, *one_a)
    got2, keep2 = sync((got2, keep2))

    def first_sums(keep, got):
        return over_y(add16(keep[2:4], got[2:4])), over_x(add16(keep[6:8], got[6:8]))

    def second_sums(keep, got, one):
        return over_x(add16(keep[1], got[1], one[0][1])), over_y(add16(keep[5], got[5], one[1][1]))

    def whole_sum(keep, got, one, two):
        return jnp.stack([add16(keep[0], got[0], one[0][0], two[0]), add16(keep[4], got[4], one[1][0], two[1])])

    one_2 = first_sums(keep2, got2)
    gps = jnp.concatenate([gp_a[:local], gp_b[:local]], axis=1).reshape(local, 4, 4, rows)
    gps = gps[:, :, jnp.array([0, 2, 1, 3])].reshape(local, owners, rows).transpose(1, 0, 2)
    gps = gps[jnp.arange(owners) ^ place]
    sum1 = layer_sum(keep_a, got_a, one_a, two_a, 1).astype(BF)
    one_2, two_a, gps, sum1 = sync((one_2, two_a, gps, sum1))

    one_3, two_2 = first_sums(keep3, got3), second_sums(keep2, got2, one_2)
    from1 = over_z(sum1)
    grad_gate, grad_up = weight_grads([xs_a, xs_b], [hs_a, hs_b], hid, 2 * hid, 2, w_gate.shape, "grad_in")
    one_3, two_2, from1, grad_gate, grad_up = sync((one_3, two_2, from1, grad_gate, grad_up))

    two_3 = second_sums(keep3, got3, one_3)
    step = leap(whole_sum(keep2, got2, one_2, two_2))
    back = lax.all_to_all(gps, "dp", 0, 0, tiled=True)
    two_3, step, back = sync((two_3, step, back))

    sum3 = whole_sum(keep3, got3, one_3, two_3)
    ends, inner = end_to_end(sum3), across(add16(sum3, step))
    other_back = over_y(back)
    (grad_down,) = weight_grads([cs_a, cs_b], [hs_a, hs_b], 0, hid, 1, w_down.shape, "grad_down")
    ends, inner, other_back, grad_down = sync((ends, inner, other_back, grad_down))
    own = layer_sum(keep_a, got_a, one_a, two_a, 0)
    result = add16(own, from1, jnp.where(middle, inner, add16(step, ends)))

    back = (back + other_back).reshape(experts, rows).T
    grad_probs = jnp.sum(jnp.where(onehot, back[:, None, :], 0.0), axis=2)
    return result[0], result[1], grad_probs, grad_gate, grad_up, grad_down


def body_any(tokens, routes, probs, w_gate, w_up, w_down, cotangent):
    rows, width = tokens.shape
    half = width // 2
    local, _, hid = w_gate.shape
    owners = lax.axis_size("dp")
    experts = local * owners
    parts = max(1, rows * owners // 2048)
    step = rows // parts
    table, onehot = dense_probs(routes, probs, experts)
    arrived = lax.all_to_all(table.reshape(rows, owners, local).transpose(1, 0, 2), "dp", 0, 0, tiled=True)
    def one_part(grads, inputs):
        own_x, own_c, own_p = inputs
        x = lax.all_gather(own_x, "dp", axis=0, tiled=True)
        c = lax.all_gather(lax.all_gather(own_c, "dp", axis=0, tiled=True), "col", axis=1, tiled=True)
        p = own_p.reshape(owners * step, local).T[:, :, None]
        gate = jnp.einsum("td,ldh->lth", x, w_gate, preferred_element_type=F32)
        up = jnp.einsum("td,ldh->lth", x, w_up, preferred_element_type=F32)
        q = jnp.einsum("td,lhd->lth", c, w_down, preferred_element_type=F32)
        s = jax.nn.sigmoid(gate)
        silu = gate * s
        hidden = (silu * up).astype(BF).astype(F32)
        dh = p * q
        hp = (p * hidden).astype(BF)
        dg = (dh * up * s * (1.0 + gate * (1.0 - s))).astype(BF)
        du = (dh * silu).astype(BF)
        m = jnp.einsum("lth,lhd->td", hp, w_down, preferred_element_type=F32).astype(BF)
        g = (jnp.einsum("lth,ldh->td", dg, w_gate, preferred_element_type=F32)
             + jnp.einsum("lth,ldh->td", du, w_up, preferred_element_type=F32)).astype(BF)
        sums = []
        for part in (m, g):
            part = lax.psum_scatter(part, "dp", scatter_dimension=0, tiled=True)
            sums.append(lax.psum_scatter(part, "col", scatter_dimension=1, tiled=True))
        new = (jnp.einsum("td,lth->ldh", x, dg, preferred_element_type=F32),
               jnp.einsum("td,lth->ldh", x, du, preferred_element_type=F32),
               jnp.einsum("lth,td->lhd", hp, c, preferred_element_type=F32))
        grads = tuple(a + b for a, b in zip(grads, new))
        return grads, (*sums, jnp.sum(hidden * q, axis=2))

    zeros = tuple(jnp.zeros(w.shape, F32) for w in (w_gate, w_up, w_down))
    arrived = arrived.reshape(owners, parts, step, local).transpose(1, 0, 2, 3)
    grads, (mixed, grad_tokens, gps) = lax.scan(
        one_part, zeros,
        (tokens.reshape(parts, step, width), cotangent.reshape(parts, step, half), arrived))
    back = gps.reshape(parts, local, owners, step).transpose(2, 0, 3, 1).reshape(owners, rows, local)
    back = lax.all_to_all(back, "dp", 0, 0, tiled=True)
    back = lax.psum(back.transpose(1, 0, 2).reshape(rows, experts), "col")
    grad_probs = jnp.sum(jnp.where(onehot, back[:, None, :], 0.0), axis=2)
    return (mixed.reshape(rows, half), grad_tokens.reshape(rows, half), grad_probs,
            *(v.astype(BF) for v in grads))


def solution(mesh):
    body = body16 if mesh.shape["dp"] == 16 and mesh.shape["col"] == 2 else body_any
    return jax.shard_map(
        body,
        mesh=mesh,
        in_specs=(
            P("dp", None),
            P("dp", None),
            P("dp", None),
            P("dp", None, "col"),
            P("dp", None, "col"),
            P("dp", "col", None),
            P("dp", "col"),
        ),
        out_specs=(
            P("dp", "col"),
            P("dp", "col"),
            P("dp", None),
            P("dp", None, "col"),
            P("dp", None, "col"),
            P("dp", "col", None),
        ),
        check_vma=False,
    )
```
